768 devices in a mesh: sfc: 384 (over z, y, x), grp: 2 (over core).
Axes of the slice: x: 4, y: 8, z: 12, core: 2. Of those that a mesh axis runs over, the one named last changes fastest.
Arguments:
- ocean_field: float32 [16, 1572864], P(None, ('sfc', 'grp')), may hold values from -6 to 6
- atm_field: float32 [16, 1572864], P('grp', 'sfc'), may hold values from -6 to 6
- tile_weights: float32 [18432, 64, 128], P(('sfc', 'grp')), may hold values from -0.75 to 0.75
- tile_source: int32 [18432], P(('sfc', 'grp')), may hold values from 0 to 31
- tile_target: int32 [18432], P(('sfc', 'grp')), may hold values from 0 to 95, as said below
- tile_count: int32 [768], P(('sfc', 'grp')), may hold values from 12 to 24, as said below
- ocean_adjacency: int32 [2, 1572864], P(None, ('sfc', 'grp')), may hold values from 0 to 2047
- atm_adjacency: int32 [2, 1572864], P(None, 'sfc'), may hold values from 0 to 4095
Outputs:
- atm_from_ocean: float32 [16, 1572864], P('grp', 'sfc')
- ocean_from_atm: float32 [16, 1572864], P(None, ('sfc', 'grp'))
The draws below stay inside these ranges and needn't reach their ends.
Inputs may be any that keep to these rules, and one draw needn't show every extreme that they name: `tile_count`: every device has 12 or more live tiles, and some device has exactly 24. `tile_target`: the tiles of a device with grp index g target blocks from a run of max(2, 2 * 4096 // 64 // 2) blocks that starts at g * 64 // 2; each device's first tile slot targets the last block of its run.
All inputs are finite; a program needn't handle non-finite values.
Results may differ from the reference program's by a relative error of at most 0.0003.
Values sent between devices are 32-bit elements; how exact they have to be, the bound alone decides.
A program may use at most 32 MiB of HBM per device.

```python
import jax
import jax.numpy as jnp
from jax import lax

C = 16
TB = 64
OCN_DEV = 2048
ATM_DEV = 4096
TILE_CAP = 24
NO = 1572864
NA = 1572864
NTILES = 18432
N_SFC = 384
N_GRP = 2
DEVICES = 768


def draw_tile_count(key, part):
    first_key, second_key = jax.random.split(jax.random.fold_in(key, 17))
    counts = jax.random.randint(first_key, (DEVICES,), TILE_CAP // 2, TILE_CAP + 1)
    fullest = jax.random.randint(second_key, (), 0, DEVICES)
    return jnp.where(jnp.arange(DEVICES) == fullest, TILE_CAP, counts).astype(jnp.int32)


def draw_tile_target(key, part):
    slot_index = jnp.arange(NTILES, dtype=jnp.int32)
    device = slot_index // TILE_CAP
    group_index = device % N_GRP
    own_blocks = ATM_DEV // TB
    run_length = max(2, 2 * own_blocks // N_GRP)
    base_block = group_index * own_blocks // N_GRP
    offsets = jax.random.randint(jax.random.fold_in(key, 29), (NTILES,), 0, run_length)
    offsets = jnp.where(slot_index % TILE_CAP == 0, run_length - 1, offsets)
    return (base_block + offsets).astype(jnp.int32)


def plant(drawn, own_key, low, largest):
    longest = drawn.shape.index(max(drawn.shape))
    spots = []
    for shift in (0, 1):
        where = [jax.random.randint(jax.random.fold_in(own_key, axis), (), 0, length) for axis, length in enumerate(drawn.shape)]
        where[longest] = (where[longest] + shift) % drawn.shape[longest]
        spots.append(tuple(where))
    return drawn.at[spots[0]].set(low).at[spots[1]].set(largest)


def level_of(rng, extent, cuts, least, largest):
    level = 1.0
    for position, parts in cuts:
        heights = jax.random.uniform(jax.random.fold_in(jax.random.fold_in(rng, 6), position), (parts,), jnp.float32, least / len(cuts), largest / len(cuts))
        level = level * jnp.repeat(jnp.exp(heights), extent[position] // parts).reshape((-1,) + (1,) * (len(extent) - 1 - position))
    return level


def gaussian(rng, dims, scale, most, pieces=(), kind=jnp.bfloat16):
    result = scale * jax.random.normal(rng, dims, jnp.float32)
    if pieces:
        result = result * level_of(rng, dims, pieces, -0.22, 0.18)
    return jnp.clip(result, -most, most).astype(kind)


def setup_inputs(seed: int = 0) -> dict:
    splits = jax.random.split(jax.random.key(seed), 9)
    return {
        "ocean_field": gaussian(splits[0], (C, NO), 1.0, 6.0, ((1, 768),), jnp.float32),
        "atm_field": gaussian(splits[1], (C, NA), 1.0, 6.0, ((0, 2), (1, 384)), jnp.float32),
        "tile_weights": gaussian(splits[2], (NTILES, TB, 2 * TB), TB ** -0.5, 0.75, ((0, 768),), jnp.float32),
        "tile_source": plant(jax.random.randint(splits[3], (NTILES,), 0, OCN_DEV // TB), jax.random.fold_in(splits[3], 1), 0, (OCN_DEV // TB) - 1).astype(jnp.int32),
        "tile_target": draw_tile_target(jax.random.fold_in(splits[8], 71), 0),
        "tile_count": draw_tile_count(jax.random.fold_in(splits[8], 71), 0),
        "ocean_adjacency": plant(jax.random.randint(splits[6], (2, NO), 0, OCN_DEV), jax.random.fold_in(splits[6], 1), 0, OCN_DEV - 1).astype(jnp.int32),
        "atm_adjacency": plant(jax.random.randint(splits[7], (2, NA), 0, ATM_DEV), jax.random.fold_in(splits[7], 1), 0, ATM_DEV - 1).astype(jnp.int32),
    }


HIGH = lax.Precision.HIGHEST


def curve_slope(field, adjacency, groups, width):
    shaped = field.reshape(field.shape[0], groups, width)
    links = adjacency.reshape(2, groups, width)
    ahead = jnp.take_along_axis(shaped, links[1][None], axis=2)
    behind = jnp.take_along_axis(shaped, links[0][None], axis=2)
    return (ahead - behind).reshape(field.shape[0], groups * width)


def reference(ocean_field, atm_field, tile_weights, tile_source, tile_target, tile_count, ocean_adjacency, atm_adjacency):
    devices = N_SFC * N_GRP
    ocean_blocks = OCN_DEV // TB
    window_blocks = 2 * ATM_DEV // TB
    ocean_slope = curve_slope(ocean_field, ocean_adjacency, devices, OCN_DEV)
    atm_slope = curve_slope(atm_field, atm_adjacency, N_SFC, ATM_DEV)
    ocean_dev = jnp.transpose(ocean_field.reshape(C, devices, ocean_blocks, TB), (1, 0, 2, 3))
    slope_dev = jnp.transpose(ocean_slope.reshape(C, devices, ocean_blocks, TB), (1, 0, 2, 3))
    weights = tile_weights.reshape(devices, TILE_CAP, TB, 2 * TB)
    sources = tile_source.reshape(devices, TILE_CAP)
    targets = tile_target.reshape(devices, TILE_CAP)
    atm_padded = jnp.concatenate([atm_field, jnp.zeros((C, ATM_DEV), jnp.float32)], axis=1)
    slope_padded = jnp.concatenate([atm_slope, jnp.zeros((C, ATM_DEV), jnp.float32)], axis=1)
    slots = jnp.arange(TILE_CAP, dtype=jnp.int32)

    def forward(inputs):
        weight, source, target, live, fields, slopes = inputs
        live_mask = (slots < live).astype(jnp.float32)
        picked = fields[:, source]
        picked_slope = slopes[:, source]
        contrib = jnp.einsum('tij,ctj->cti', weight[:, :, :TB], picked, precision=HIGH) + jnp.einsum('tij,ctj->cti', weight[:, :, TB:], picked_slope, precision=HIGH)
        onehot = (target[:, None] == jnp.arange(window_blocks, dtype=jnp.int32)[None]).astype(jnp.float32) * live_mask[:, None]
        return jnp.einsum('cti,tb->cbi', contrib, onehot, precision=HIGH).reshape(C, 2 * ATM_DEV)

    windows = lax.map(forward, (weights, sources, targets, tile_count, ocean_dev, slope_dev))
    summed = windows.reshape(N_SFC, N_GRP, C, 2 * ATM_DEV).sum(axis=1)
    lower = summed[:, :, :ATM_DEV]
    upper = jnp.concatenate([jnp.zeros((1, C, ATM_DEV), jnp.float32), summed[:-1, :, ATM_DEV:]], axis=0)
    atm_from_ocean = jnp.transpose(lower + upper, (1, 0, 2)).reshape(C, NA)

    def backward(inputs):
        device, weight, source, target, live = inputs
        live_mask = (slots < live).astype(jnp.float32)
        start = (device // N_GRP) * ATM_DEV
        window = lax.dynamic_slice_in_dim(atm_padded, start, 2 * ATM_DEV, 1).reshape(C, window_blocks, TB)
        window_slope = lax.dynamic_slice_in_dim(slope_padded, start, 2 * ATM_DEV, 1).reshape(C, window_blocks, TB)
        contrib = jnp.einsum('tij,cti->ctj', weight[:, :, :TB], window[:, target], precision=HIGH) + jnp.einsum('tij,cti->ctj', weight[:, :, TB:], window_slope[:, target], precision=HIGH)
        onehot = (source[:, None] == jnp.arange(ocean_blocks, dtype=jnp.int32)[None]).astype(jnp.float32) * live_mask[:, None]
        return jnp.einsum('ctj,to->coj', contrib, onehot, precision=HIGH).reshape(C, OCN_DEV)

    backs = lax.map(backward, (jnp.arange(devices, dtype=jnp.int32), weights, sources, targets, tile_count))
    ocean_from_atm = jnp.transpose(backs, (1, 0, 2)).reshape(C, NO)
    return atm_from_ocean, ocean_from_atm
```

```python
import functools

import jax
import jax.numpy as jnp
from jax import lax
from jax.experimental import pallas as pl
from jax.experimental.pallas import tpu as pltpu
from jax.sharding import PartitionSpec as P

TB = 64
LANES = 128
MESH = pl.DeviceIdType.MESH
F32 = jnp.float32
BF16 = jnp.bfloat16


def roll_half(x):
    return pltpu.roll(x, TB, x.ndim - 1)


def pick_lanes(load, count, index):
    low = index & (LANES - 1)
    high = index >> 7
    bits = [(high >> b) & 1 == 1 for b in range((count - 1).bit_length())]

    def tree(first, level):
        if level < 0:
            return jnp.take_along_axis(load(first), low, axis=1, mode="promise_in_bounds")
        left = tree(first, level - 1)
        right = tree(first + (1 << level), level - 1)
        return jnp.where(bits[level], right, left)

    return tree(0, len(bits) - 1)


def field_and_slope(load, count, ahead, behind, here, odd):
    rows = here.shape[0]
    half = (lax.broadcasted_iota(jnp.int32, (rows, LANES), 1) >= TB).astype(jnp.int32)
    own = half == odd
    ahead = jnp.broadcast_to(ahead, (rows, LANES))
    behind = jnp.broadcast_to(behind, (rows, LANES))
    index = jnp.where(own, ahead, roll_half(behind))
    got = pick_lanes(load, count, index)
    mixed = jnp.where(own, here, roll_half(got) - got)
    return jnp.where(half * 0 + odd == 0, mixed, roll_half(mixed))


def split(x):
    high = x.astype(BF16)
    return high, (x - high.astype(F32)).astype(BF16)


def both_halves(product):
    rows = product.shape[0] // 2
    added = product[:rows] + product[rows:]
    return added + roll_half(added)


def kernel(
    n_sfc,
    ocean_hbm,
    atm_hbm,
    weights_hbm,
    source_hbm,
    target_hbm,
    count_hbm,
    ocean_adj_hbm,
    atm_adj_hbm,
    atm_out,
    ocean_out,
    ocean,
    fields,
    ocean_adj,
    atm_adj,
    weights,
    source,
    target,
    count,
    picked,
    terms,
    partial,
    from_partner,
    from_behind,
    ocean_tiles,
    ocean_links,
    field_tiles,
    atm_links,
    local_sem,
    send_sem,
    recv_sem,
):
    s = lax.axis_index("sfc")
    g = lax.axis_index("grp")
    columns, ocean_cells = ocean.shape
    half_columns, atm_cells = atm_hbm.shape
    tiles = weights.shape[0]
    half_cells = atm_cells // 2
    following = lax.rem(s + 1, n_sfc)
    before = lax.rem(s + n_sfc - 1, n_sfc)

    def local(src, dst, number):
        copy = pltpu.make_async_copy(src, dst, local_sem.at[number])
        copy.start()
        return copy

    def remote(src, dst, number, sfc, grp):
        return pltpu.make_async_remote_copy(
            src_ref=src,
            dst_ref=dst,
            send_sem=send_sem.at[number],
            recv_sem=recv_sem.at[number],
            device_id={"sfc": sfc, "grp": grp},
            device_id_type=MESH,
        )

    barrier = pltpu.get_barrier_semaphore()

    def greet(sfc, grp):
        pl.semaphore_signal(
            barrier, inc=1, device_id={"sfc": sfc, "grp": grp}, device_id_type=MESH
        )

    greet(s, 1 - g)
    greet(before, 1)

    @pl.when(g == 1)
    def _():
        greet(following, 0)
        greet(following, 1)

    small = [
        local(source_hbm, source, 0),
        local(target_hbm, target, 1),
        local(count_hbm, count, 2),
        local(ocean_adj_hbm, ocean_adj, 3),
        local(ocean_hbm, ocean, 4),
    ]
    weights_copy = local(weights_hbm, weights, 5)
    later = [
        local(atm_hbm, fields.at[0, pl.ds(pl.multiple_of(half_columns * g, 8), half_columns)], 6),
        local(atm_adj_hbm, atm_adj.at[0], 7),
    ]

    @pl.when(g == 0)
    def _():
        pl.semaphore_wait(barrier, 2)

    @pl.when(g == 1)
    def _():
        pl.semaphore_wait(barrier, 4)

    def partner_field(part):
        return remote(
            atm_hbm, fields.at[0, half_columns * part : half_columns * (part + 1)], 0, s, 1 - part
        )

    def before_field(part):
        return remote(
            atm_hbm,
            fields.at[1, half_columns * part : half_columns * (part + 1)],
            1 + part,
            before,
            1,
        )

    def before_adjacency():
        cells = pl.ds(0, half_cells)
        return remote(atm_adj_hbm.at[:, cells], atm_adj.at[1, :, cells], 3, before, 1)

    @pl.when(g == 0)
    def _():
        before_adjacency().start()
        before_field(0).start()
        partner_field(0).start()

    @pl.when(g == 1)
    def _():
        before_field(1).start()
        partner_field(1).start()

    for copy in small:
        copy.wait()

    live = count[0]
    for k in range(ocean_cells // LANES):
        ocean_tiles[k] = ocean[:, k * LANES : (k + 1) * LANES]
        ocean_links[k] = ocean_adj[:, k * LANES : (k + 1) * LANES]

    def pick_ocean(t, carry):
        block = source[t]
        cells = block >> 1
        x = field_and_slope(
            lambda k: ocean[:, k * LANES : (k + 1) * LANES],
            ocean_cells // LANES,
            ocean_links[cells, 1:2],
            ocean_links[cells, 0:1],
            ocean_tiles[cells],
            block & 1,
        )
        high, low = split(x)
        picked[t, :columns] = high
        picked[t, columns:] = low
        return carry

    lax.fori_loop(0, tiles, pick_ocean, 0)
    weights_copy.wait()

    def forward(t, carry):
        high, low = split(weights[t])
        both = jnp.concatenate([high, low], axis=0)
        product = lax.dot_general(
            picked[t], both, (((1,), (1,)), ((), ())), preferred_element_type=F32
        )
        terms[t] = both_halves(product)
        return carry

    def each_tile(body, group):
        def step(i, carry):
            for j in range(group):
                body(i * group + j, carry)
            return carry

        lax.fori_loop(0, tiles // group, step, 0)

    each_tile(forward, 4)

    half = (lax.broadcasted_iota(jnp.int32, (columns, LANES), 1) >= TB).astype(jnp.int32)

    def gathered_sum(p, blocks):
        here = half + 2 * p
        total = jnp.zeros((columns, LANES), F32)
        for t in range(tiles):
            total = total + jnp.where(here == blocks[t], terms[t], 0.0)
        return total

    run_start = g * (half_cells // TB)
    target_run = [
        jnp.where(t < live, target[t] - run_start, -1) for t in range(tiles)
    ]

    def add_targets(p, carry):
        cells = pl.ds(pl.multiple_of(p * LANES, LANES), LANES)
        partial[:, cells] = gathered_sum(p, target_run)
        return carry

    low_cells, high_cells = pl.ds(0, half_cells), pl.ds(half_cells, half_cells)
    low_columns, high_columns = pl.ds(0, half_columns), pl.ds(half_columns, half_columns)
    mid = half_cells // LANES

    def following_sum(part):
        return remote(
            partial.at[pl.ds(half_columns * part, half_columns), high_cells],
            from_behind,
            5 + part,
            following,
            part,
        )

    def partner_sum(part):
        if part == 0:
            return remote(partial.at[high_columns], from_partner, 4, s, 1)
        return remote(
            partial.at[low_columns, low_cells], from_partner.at[:, low_cells], 4, s, 0
        )

    lax.fori_loop(mid, 2 * mid, add_targets, 0)

    @pl.when(g == 1)
    def _():
        following_sum(0).start()
        following_sum(1).start()

    lax.fori_loop(0, mid, add_targets, 0)

    @pl.when(g == 0)
    def _():
        partner_sum(0).start()

    @pl.when(g == 1)
    def _():
        partner_sum(1).start()

    for copy in later:
        copy.wait()

    @pl.when(g == 0)
    def _():
        partner_field(1).wait_recv()

    @pl.when(g == 1)
    def _():
        partner_field(0).wait_recv()
        before_field(0).wait_recv()
        before_field(1).wait_recv()
        before_adjacency().wait_recv()

    atm_tiles = atm_cells // LANES
    for k in range(2 * atm_tiles):
        lanes = pl.ds(k % atm_tiles * LANES, LANES)
        field_tiles[k] = fields[k // atm_tiles, :, lanes]
        atm_links[k] = atm_adj[k // atm_tiles, :, lanes]

    atm_blocks = atm_cells // TB
    last_block = atm_blocks - 1 + g * (atm_blocks // 2)
    is_last = s == n_sfc - 1

    def pick_atm(t, carry):
        window_block = jnp.minimum(target[t], last_block)
        past = (window_block >= atm_blocks).astype(jnp.int32)
        block = window_block - past * atm_blocks
        cells = block >> 1
        x = field_and_slope(
            lambda k: field_tiles[past * (atm_cells // LANES) + k],
            atm_cells // LANES,
            atm_links[past * (atm_cells // LANES) + cells, 1:2],
            atm_links[past * (atm_cells // LANES) + cells, 0:1],
            field_tiles[past * (atm_cells // LANES) + cells],
            block & 1,
        )
        x = jnp.where(half * 0 + past * is_last.astype(jnp.int32) == 0, x, 0.0)
        high, low = split(x)
        picked[t, :columns] = high
        picked[t, columns:] = low
        return carry

    lax.fori_loop(0, tiles, pick_atm, 0)

    def backward(t, carry):
        weight = weights[t]
        lower = lax.broadcasted_iota(jnp.int32, weight.shape, 1) < TB
        high = weight.astype(BF16).astype(F32)
        low = weight - high
        turned = roll_half(jnp.where(lower, low, high))
        both = jnp.concatenate(
            [jnp.where(lower, high, turned), jnp.where(lower, turned, low)], axis=0
        ).astype(BF16)
        terms[t] = both_halves(jnp.dot(picked[t], both, preferred_element_type=F32))
        return carry

    each_tile(backward, 4)
    source_run = [jnp.where(t < live, source[t], -1) for t in range(tiles)]

    def add_sources(p, carry):
        cells = pl.ds(pl.multiple_of(p * LANES, LANES), LANES)
        ocean_out[:, cells] = gathered_sum(p, source_run)
        return carry

    lax.fori_loop(0, ocean_cells // LANES, add_sources, 0)

    @pl.when(g == 0)
    def _():
        partner_sum(1).wait_recv()
        following_sum(0).wait_recv()
        behind = jnp.where(s == 0, 0.0, from_behind[...])
        atm_out[:, low_cells] = partial[low_columns, low_cells] + behind
        atm_out[:, high_cells] = partial[low_columns, high_cells] + from_partner[:, low_cells]

    @pl.when(g == 1)
    def _():
        partner_sum(0).wait_recv()
        following_sum(1).wait_recv()
        behind = jnp.where(s == 0, 0.0, from_behind[...])
        atm_out[:, low_cells] = from_partner[:, low_cells] + behind
        atm_out[:, high_cells] = from_partner[:, high_cells] + partial[high_columns, low_cells]

    @pl.when(g == 0)
    def _():
        before_adjacency().wait_send()
        before_field(0).wait_send()
        partner_field(0).wait_send()
        partner_sum(0).wait_send()

    @pl.when(g == 1)
    def _():
        before_field(1).wait_send()
        partner_field(1).wait_send()
        partner_sum(1).wait_send()
        following_sum(0).wait_send()
        following_sum(1).wait_send()


def per_device(
    n_sfc,
    ocean_field,
    atm_field,
    tile_weights,
    tile_source,
    tile_target,
    tile_count,
    ocean_adjacency,
    atm_adjacency,
):
    columns, ocean_cells = ocean_field.shape
    half_columns, atm_cells = atm_field.shape
    tiles = tile_source.shape[0]
    return pl.pallas_call(
        functools.partial(kernel, n_sfc),
        out_shape=(
            jax.ShapeDtypeStruct((half_columns, atm_cells), F32),
            jax.ShapeDtypeStruct((columns, ocean_cells), F32),
        ),
        in_specs=[pl.BlockSpec(memory_space=pltpu.HBM)] * 8,
        out_specs=(
            pl.BlockSpec(memory_space=pltpu.VMEM),
            pl.BlockSpec(memory_space=pltpu.VMEM),
        ),
        scratch_shapes=[
            pltpu.VMEM((columns, ocean_cells), F32),
            pltpu.VMEM((2, columns, atm_cells), F32),
            pltpu.VMEM((2, ocean_cells), jnp.int32),
            pltpu.VMEM((2, 2, atm_cells), jnp.int32),
            pltpu.VMEM(tile_weights.shape, F32),
            pltpu.SMEM((tiles,), jnp.int32),
            pltpu.SMEM((tiles,), jnp.int32),
            pltpu.SMEM((1,), jnp.int32),
            pltpu.VMEM((tiles, 2 * columns, LANES), BF16),
            pltpu.VMEM((tiles, columns, LANES), F32),
            pltpu.VMEM((columns, atm_cells), F32),
            pltpu.VMEM((half_columns, atm_cells), F32),
            pltpu.VMEM((half_columns, atm_cells // 2), F32),
            pltpu.VMEM((ocean_cells // LANES, columns, LANES), F32),
            pltpu.VMEM((ocean_cells // LANES, 2, LANES), jnp.int32),
            pltpu.VMEM((2 * atm_cells // LANES, columns, LANES), F32),
            pltpu.VMEM((2 * atm_cells // LANES, 2, LANES), jnp.int32),
            pltpu.SemaphoreType.DMA((8,)),
            pltpu.SemaphoreType.DMA((7,)),
            pltpu.SemaphoreType.DMA((7,)),
        ],
        compiler_params=pltpu.CompilerParams(
            collective_id=0, has_side_effects=True, vmem_limit_bytes=63 * 1024 * 1024
        ),
    )(
        ocean_field,
        atm_field,
        tile_weights,
        tile_source,
        tile_target,
        tile_count,
        ocean_adjacency,
        atm_adjacency,
    )


def solution(mesh):
    return jax.shard_map(
        functools.partial(per_device, mesh.shape["sfc"]),
        mesh=mesh,
        in_specs=(
            P(None, ("sfc", "grp")),
            P("grp", "sfc"),
            P(("sfc", "grp"), None, None),
            P(("sfc", "grp")),
            P(("sfc", "grp")),
            P(("sfc", "grp")),
            P(None, ("sfc", "grp")),
            P(None, "sfc"),
        ),
        out_specs=(P("grp", "sfc"), P(None, ("sfc", "grp"))),
        check_vma=False,
    )
```

```python
import functools

import jax
import jax.numpy as jnp
from jax import lax
from jax.experimental import pallas as pl
from jax.experimental.pallas import tpu as pltpu
from jax.sharding import PartitionSpec as P

TB = 64
LANES = 128
ROWS = 8
GATHER = 24
JOIN = 24
VLIM = 63 * 1024 * 1024
MESH = pl.DeviceIdType.MESH
F32 = jnp.float32
BF16 = jnp.bfloat16


def roll_half(x):
    return pltpu.roll(x, TB, x.ndim - 1)


def lower_lanes(rows):
    return lax.broadcasted_iota(jnp.int32, (rows, LANES), 1) < TB


def pick_lanes(load, count, index):
    low = index & (LANES - 1)
    high = index >> 7
    bits = [(high >> b) & 1 == 1 for b in range((count - 1).bit_length())]

    def tree(first, level):
        if level < 0:
            return jnp.take_along_axis(load(first), low, axis=1, mode="promise_in_bounds")
        left = tree(first, level - 1)
        right = tree(first + (1 << level), level - 1)
        return jnp.where(bits[level], right, left)

    return tree(0, len(bits) - 1)


def stacked(x):
    high = x.astype(BF16).astype(F32)
    return jnp.concatenate([high, x - high], axis=0).astype(BF16)


def block_links(links):
    ahead = jnp.broadcast_to(links[1:2], (ROWS, LANES))
    behind = jnp.broadcast_to(links[0:1], (ROWS, LANES))
    lower = lower_lanes(ROWS)
    return (
        jnp.where(lower, ahead, roll_half(behind)),
        jnp.where(lower, roll_half(ahead), behind),
    )


def each(count, group, body):
    def step(i, carry):
        for j in range(group):
            body(i * group + j)
        return carry

    if group == count:
        step(0, 0)
    else:
        lax.fori_loop(0, count // group, step, 0)


def kernel(
    n_sfc,
    ocean_hbm,
    atm_hbm,
    weights_hbm,
    source_hbm,
    target_hbm,
    count_hbm,
    ocean_adj_hbm,
    atm_adj_hbm,
    atm_out,
    ocean_out,
    ocean,
    own_fields,
    partner_fields,
    ocean_adj,
    atm_adj,
    weights,
    source,
    target,
    count,
    ocean_links,
    atm_links,
    split_weights,
    got,
    picked,
    terms,
    places,
    partial,
    from_partner,
    from_behind,
    local_sem,
    send_sem,
    recv_sem,
):
    s = lax.axis_index("sfc")
    g = lax.axis_index("grp")
    ocean_tiles = ocean.shape[1]
    atm_tiles = atm_hbm.shape[0]
    half_tiles = atm_tiles // 2
    tiles = weights.shape[0]
    has_following = s < n_sfc - 1
    has_before = s > 0
    following = jnp.minimum(s + 1, n_sfc - 1)
    before = jnp.maximum(s - 1, 0)
    sends_on = jnp.logical_and(g == 1, has_following)

    def local(src, dst, number):
        return pltpu.make_async_copy(src, dst, local_sem.at[number])

    def remote(src, dst, number, sfc, grp):
        return pltpu.make_async_remote_copy(
            src_ref=src,
            dst_ref=dst,
            send_sem=send_sem.at[number],
            recv_sem=recv_sem.at[number],
            device_id={"sfc": sfc, "grp": grp},
            device_id_type=MESH,
        )

    barrier = pltpu.get_barrier_semaphore()

    def greet(sfc, grp):
        pl.semaphore_signal(
            barrier, inc=1, device_id={"sfc": sfc, "grp": grp}, device_id_type=MESH
        )

    greet(s, 1 - g)

    @pl.when(has_before)
    def _():
        greet(before, 1)

    @pl.when(sends_on)
    def _():
        greet(following, 0)
        greet(following, 1)

    small_copies = [
        local(source_hbm, source, 0),
        local(target_hbm, target, 1),
        local(count_hbm, count, 2),
        local(ocean_adj_hbm, ocean_adj, 3),
        local(ocean_hbm, ocean, 4),
    ]
    weights_copy = local(weights_hbm, weights, 5)
    field_copy = local(atm_hbm, own_fields.at[0], 6)
    low_adj_copy = local(atm_adj_hbm.at[pl.ds(g * half_tiles, half_tiles)], atm_adj.at[0], 7)
    high_adj_copy = local(atm_adj_hbm.at[pl.ds(half_tiles, half_tiles)], atm_adj.at[1], 8)
    for copy in small_copies + [weights_copy, field_copy, low_adj_copy]:
        copy.start()

    @pl.when(g == 0)
    def _():
        high_adj_copy.start()

    peers = 1 + has_before.astype(jnp.int32) + 2 * sends_on.astype(jnp.int32)
    pl.semaphore_wait(barrier, peers)

    def partner_field(part):
        return remote(atm_hbm, partner_fields.at[0], 0, s, 1 - part)

    def before_field(part):
        landing = own_fields if part == 1 else partner_fields
        return remote(atm_hbm, landing.at[1], 1 + part, before, 1)

    def before_adjacency():
        return remote(atm_adj_hbm.at[pl.ds(0, half_tiles)], atm_adj.at[1], 3, before, 1)

    @pl.when(g == 0)
    def _():
        partner_field(0).start()

        @pl.when(has_before)
        def _():
            before_adjacency().start()
            before_field(0).start()

    @pl.when(g == 1)
    def _():
        partner_field(1).start()

        @pl.when(has_before)
        def _():
            before_field(1).start()

    for copy in small_copies:
        copy.wait()

    live = count[0]
    upper = 1 - lower_lanes(ROWS).astype(jnp.int32)

    def store_links(links, first, adjacency, number):
        for k in range(number):
            even, odd = block_links(adjacency[k])
            links[first + 2 * k] = even
            links[first + 2 * k + 1] = odd

    def store_places(block_of):
        for t in range(tiles):
            places[t] = jnp.where(t < live, block_of(t), -2) - upper

    def scatter(out, part, number):
        group = 4

        def step(i, carry):
            sums = [jnp.zeros((ROWS, LANES), F32) for _ in range(group)]
            for t in range(tiles):
                place, term = places[t], terms[t]
                for j in range(group):
                    first = 2 * (i * group + j)
                    sums[j] = sums[j] + jnp.where(place == first, term, 0.0)
            for j in range(group):
                out[part, i * group + j] = sums[j]
            return carry

        lax.fori_loop(0, number // group, step, 0)

    def pick_ocean(part):
        def gather(t):
            got[t] = pick_lanes(lambda k: ocean[part, k], ocean_tiles, ocean_links[source[t]])

        each(tiles, GATHER, gather)

        def join(t):
            block = source[t]
            tile = ocean[part, block >> 1]
            field = jnp.where(upper * 0 + (block & 1) == 0, tile, roll_half(tile))
            slope = roll_half(got[t]) - got[t]
            picked[t, : 2 * ROWS] = stacked(jnp.where(lower_lanes(ROWS), field, slope))

        each(tiles, JOIN, join)

    def forward():
        for t in range(tiles):
            product = lax.dot_general(
                picked[t, : 2 * ROWS],
                split_weights[t],
                (((1,), (1,)), ((), ())),
                preferred_element_type=F32,
            )
            added = product[:ROWS] + product[ROWS:]
            terms[t] = added + roll_half(added)

    run_start = g * half_tiles * 2
    store_links(ocean_links, 0, ocean_adj, ocean_tiles)
    store_places(lambda t: target[t] - run_start)
    pick_ocean(1 - g)
    weights_copy.wait()

    def split(t):
        split_weights[t] = stacked(weights[t])

    each(tiles, 4, split)
    forward()
    scatter(partial, 0, atm_tiles)

    low_half, high_half = pl.ds(0, half_tiles), pl.ds(half_tiles, half_tiles)

    def following_sum(part):
        return remote(partial.at[part, high_half], from_behind, 5 + part, following, part)

    def partner_sum(part):
        if part == 0:
            return remote(partial.at[0], from_partner, 4, s, 1)
        return remote(partial.at[0, low_half], from_partner.at[low_half], 4, s, 0)

    @pl.when(g == 0)
    def _():
        partner_sum(0).start()

    @pl.when(g == 1)
    def _():
        partner_sum(1).start()

    @pl.when(sends_on)
    def _():
        following_sum(0).start()

    pick_ocean(g)
    forward()
    scatter(partial, 1, atm_tiles)

    @pl.when(sends_on)
    def _():
        following_sum(1).start()

    is_last = jnp.logical_not(has_following).astype(jnp.int32)

    def pick_atm(fields):
        def place_of(t):
            block = jnp.clip(target[t] - run_start, 0, 2 * atm_tiles - 1)
            past = g * (block >= atm_tiles).astype(jnp.int32)
            return block, past

        def gather(t):
            block, past = place_of(t)
            got[t] = pick_lanes(
                lambda k: fields[past, k], atm_tiles, atm_links[block]
            )

        each(tiles, GATHER, gather)

        def join(t):
            block, past = place_of(t)
            tile = fields[past, (block + run_start - 2 * atm_tiles * past) >> 1]
            turned = roll_half(tile)
            lower = lower_lanes(ROWS)
            keep = upper * 0 + past * is_last == 0
            field = jnp.where(upper == (block & 1), tile, turned)
            ahead = roll_half(got[t]) - got[t]
            slope = jnp.where(lower, -ahead, ahead)
            picked[t, : 2 * ROWS] = stacked(jnp.where(keep, field, 0.0))
            picked[t, 2 * ROWS :] = stacked(jnp.where(keep, slope, 0.0))

        each(tiles, JOIN, join)

    def backward():
        lower = lower_lanes(ROWS)
        for t in range(tiles):
            product = jnp.dot(picked[t], split_weights[t], preferred_element_type=F32)
            field = product[:ROWS] + product[ROWS : 2 * ROWS]
            slope = product[2 * ROWS : 3 * ROWS] + product[3 * ROWS :]
            both = jnp.where(lower, field, slope)
            terms[t] = both + roll_half(both)

    low_adj_copy.wait()
    field_copy.wait()

    @pl.when(g == 0)
    def _():
        high_adj_copy.wait()

    @pl.when(sends_on)
    def _():
        before_adjacency().wait_recv()
        before_field(1).wait_recv()

    store_links(atm_links, 0, atm_adj.at[0], half_tiles)
    store_links(atm_links, 2 * half_tiles, atm_adj.at[1], half_tiles)
    store_places(lambda t: source[t])
    pick_atm(own_fields)
    backward()
    scatter(ocean_out, g, ocean_tiles)

    @pl.when(g == 0)
    def _():
        partner_field(1).wait_recv()

    @pl.when(g == 1)
    def _():
        partner_field(0).wait_recv()

    @pl.when(sends_on)
    def _():
        before_field(0).wait_recv()

    pick_atm(partner_fields)
    backward()
    scatter(ocean_out, 1 - g, ocean_tiles)

    def behind_sum():
        return jnp.where(has_before, from_behind[...], 0.0)

    @pl.when(g == 0)
    def _():
        partner_sum(1).wait_recv()

        @pl.when(has_before)
        def _():
            following_sum(0).wait_recv()

        atm_out[low_half] = partial[1, low_half] + behind_sum()
        atm_out[high_half] = partial[1, high_half] + from_partner[low_half]

    @pl.when(g == 1)
    def _():
        partner_sum(0).wait_recv()

        @pl.when(has_before)
        def _():
            following_sum(1).wait_recv()

        atm_out[low_half] = from_partner[low_half] + behind_sum()
        atm_out[high_half] = from_partner[high_half] + partial[1, low_half]

    @pl.when(g == 0)
    def _():
        partner_field(0).wait_send()
        partner_sum(0).wait_send()

        @pl.when(has_before)
        def _():
            before_adjacency().wait_send()
            before_field(0).wait_send()

    @pl.when(g == 1)
    def _():
        partner_field(1).wait_send()
        partner_sum(1).wait_send()

        @pl.when(has_before)
        def _():
            before_field(1).wait_send()

    @pl.when(sends_on)
    def _():
        following_sum(0).wait_send()
        following_sum(1).wait_send()


def as_tiles(x):
    rows, cells = x.shape
    return x.reshape(rows, cells // LANES, LANES).transpose(1, 0, 2)


def write_kernel(atm, ocean, atm_out, ocean_out, sem):
    copies = [
        pltpu.make_async_copy(atm, atm_out, sem.at[0]),
        pltpu.make_async_copy(ocean, ocean_out, sem.at[1]),
    ]
    for copy in copies:
        copy.start()
    for copy in copies:
        copy.wait()


def write_out(atm, ocean):
    return pl.pallas_call(
        write_kernel,
        out_shape=(
            jax.ShapeDtypeStruct(atm.shape, F32),
            jax.ShapeDtypeStruct(ocean.shape, F32),
        ),
        in_specs=[pl.BlockSpec(memory_space=pltpu.VMEM)] * 2,
        out_specs=[pl.BlockSpec(memory_space=pltpu.HBM)] * 2,
        scratch_shapes=[pltpu.SemaphoreType.DMA((2,))],
    )(
        pltpu.with_memory_space_constraint(atm, pltpu.VMEM),
        pltpu.with_memory_space_constraint(ocean, pltpu.VMEM),
    )


def per_device(
    n_sfc,
    ocean_field,
    atm_field,
    tile_weights,
    tile_source,
    tile_target,
    tile_count,
    ocean_adjacency,
    atm_adjacency,
):
    columns, ocean_cells = ocean_field.shape
    half_columns, atm_cells = atm_field.shape
    tiles = tile_source.shape[0]
    ocean_tiles = ocean_cells // LANES
    atm_tiles = atm_cells // LANES
    half_tiles = atm_tiles // 2
    vmem = pl.BlockSpec(memory_space=pltpu.VMEM)
    atm_out, ocean_out = pl.pallas_call(
        functools.partial(kernel, n_sfc),
        out_shape=(
            pltpu.VMEM((atm_tiles, ROWS, LANES), F32),
            pltpu.VMEM((2, ocean_tiles, ROWS, LANES), F32),
        ),
        in_specs=[pl.BlockSpec(memory_space=pltpu.HBM)] * 8,
        out_specs=(vmem, vmem),
        scratch_shapes=[
            pltpu.VMEM((2, ocean_tiles, ROWS, LANES), F32),
            pltpu.VMEM((2, atm_tiles, ROWS, LANES), F32),
            pltpu.VMEM((2, atm_tiles, ROWS, LANES), F32),
            pltpu.VMEM((ocean_tiles, 2, LANES), jnp.int32),
            pltpu.VMEM((2, half_tiles, 2, LANES), jnp.int32),
            pltpu.VMEM(tile_weights.shape, F32),
            pltpu.SMEM((tiles,), jnp.int32),
            pltpu.SMEM((tiles,), jnp.int32),
            pltpu.SMEM((1,), jnp.int32),
            pltpu.VMEM((2 * ocean_tiles, ROWS, LANES), jnp.int32),
            pltpu.VMEM((2 * atm_tiles, ROWS, LANES), jnp.int32),
            pltpu.VMEM((tiles, 2 * TB, LANES), BF16),
            pltpu.VMEM((tiles, ROWS, LANES), F32),
            pltpu.VMEM((tiles, 4 * ROWS, LANES), BF16),
            pltpu.VMEM((tiles, ROWS, LANES), F32),
            pltpu.VMEM((tiles, ROWS, LANES), jnp.int32),
            pltpu.VMEM((2, atm_tiles, ROWS, LANES), F32),
            pltpu.VMEM((atm_tiles, ROWS, LANES), F32),
            pltpu.VMEM((half_tiles, ROWS, LANES), F32),
            pltpu.SemaphoreType.DMA((9,)),
            pltpu.SemaphoreType.DMA((7,)),
            pltpu.SemaphoreType.DMA((7,)),
        ],
        compiler_params=pltpu.CompilerParams(
            collective_id=0, has_side_effects=True, vmem_limit_bytes=VLIM
        ),
    )(
        ocean_field.reshape(2, ROWS, ocean_tiles, LANES).transpose(0, 2, 1, 3),
        as_tiles(atm_field),
        tile_weights,
        tile_source,
        tile_target,
        tile_count,
        as_tiles(ocean_adjacency),
        as_tiles(atm_adjacency),
    )
    atm_out, ocean_out = write_out(atm_out, ocean_out)
    return (
        atm_out.transpose(1, 0, 2).reshape(half_columns, atm_cells),
        ocean_out.transpose(0, 2, 1, 3).reshape(columns, ocean_cells),
    )


def solution(mesh):
    return jax.shard_map(
        functools.partial(per_device, mesh.shape["sfc"]),
        mesh=mesh,
        in_specs=(
            P(None, ("sfc", "grp")),
            P("grp", "sfc"),
            P(("sfc", "grp"), None, None),
            P(("sfc", "grp")),
            P(("sfc", "grp")),
            P(("sfc", "grp")),
            P(None, ("sfc", "grp")),
            P(None, "sfc"),
        ),
        out_specs=(P("grp", "sfc"), P(None, ("sfc", "grp"))),
        check_vma=False,
    )
```

```python
import functools

import jax
import jax.numpy as jnp
from jax import lax
from jax.experimental import pallas as pl
from jax.experimental.pallas import tpu as pltpu
from jax.sharding import PartitionSpec as P

TB = 64
LANES = 128
ROWS = 8
GATHER = 24
JOIN = 24
VLIM = 63 * 1024 * 1024
MESH = pl.DeviceIdType.MESH
F32 = jnp.float32
BF16 = jnp.bfloat16


def roll_half(x):
    return pltpu.roll(x, TB, x.ndim - 1)


def lower_lanes(rows):
    return lax.broadcasted_iota(jnp.int32, (rows, LANES), 1) < TB


def pick_lanes(load, count, index):
    low = index & (LANES - 1)
    high = index >> 7
    bits = [(high >> b) & 1 == 1 for b in range((count - 1).bit_length())]

    def tree(first, level):
        if level < 0:
            return jnp.take_along_axis(load(first), low, axis=1, mode="promise_in_bounds")
        left = tree(first, level - 1)
        right = tree(first + (1 << level), level - 1)
        return jnp.where(bits[level], right, left)

    return tree(0, len(bits) - 1)


def stacked(x):
    high = x.astype(BF16).astype(F32)
    return jnp.concatenate([high, x - high], axis=0).astype(BF16)


def block_links(links):
    ahead = jnp.broadcast_to(links[1:2], (ROWS, LANES))
    behind = jnp.broadcast_to(links[0:1], (ROWS, LANES))
    lower = lower_lanes(ROWS)
    return (
        jnp.where(lower, ahead, roll_half(behind)),
        jnp.where(lower, roll_half(ahead), behind),
    )


def each(count, group, body):
    def step(i, carry):
        for j in range(group):
            body(i * group + j)
        return carry

    if group == count:
        step(0, 0)
    else:
        lax.fori_loop(0, count // group, step, 0)


def kernel(
    n_sfc,
    ocean_hbm,
    atm_hbm,
    weights_hbm,
    source_hbm,
    target_hbm,
    count_hbm,
    ocean_adj_hbm,
    atm_adj_hbm,
    atm_out,
    ocean_out,
    ocean,
    own_fields,
    partner_fields,
    ocean_adj,
    atm_adj,
    weights,
    source,
    target,
    count,
    ocean_links,
    atm_links,
    split_weights,
    got,
    picked,
    terms,
    places,
    partial,
    from_partner,
    from_behind,
    local_sem,
    send_sem,
    recv_sem,
):
    s = lax.axis_index("sfc")
    g = lax.axis_index("grp")
    ocean_tiles = ocean.shape[1]
    atm_tiles = atm_hbm.shape[0]
    half_tiles = atm_tiles // 2
    tiles = weights.shape[0]
    has_following = s < n_sfc - 1
    has_before = s > 0
    following = jnp.minimum(s + 1, n_sfc - 1)
    before = jnp.maximum(s - 1, 0)
    sends_on = jnp.logical_and(g == 1, has_following)

    def local(src, dst, number):
        return pltpu.make_async_copy(src, dst, local_sem.at[number])

    def remote(src, dst, number, sfc, grp):
        return pltpu.make_async_remote_copy(
            src_ref=src,
            dst_ref=dst,
            send_sem=send_sem.at[number],
            recv_sem=recv_sem.at[number],
            device_id={"sfc": sfc, "grp": grp},
            device_id_type=MESH,
        )

    barrier = pltpu.get_barrier_semaphore()

    def greet(sfc, grp):
        pl.semaphore_signal(
            barrier, inc=1, device_id={"sfc": sfc, "grp": grp}, device_id_type=MESH
        )

    greet(s, 1 - g)

    @pl.when(has_before)
    def _():
        greet(before, 1)

    @pl.when(sends_on)
    def _():
        greet(following, 0)
        greet(following, 1)

    small_copies = [
        local(source_hbm, source, 0),
        local(target_hbm, target, 1),
        local(count_hbm, count, 2),
        local(ocean_adj_hbm, ocean_adj, 3),
        local(ocean_hbm, ocean, 4),
    ]
    weights_copy = local(weights_hbm, weights, 5)
    field_copy = local(atm_hbm, own_fields.at[0], 6)
    low_adj_copy = local(atm_adj_hbm.at[pl.ds(g * half_tiles, half_tiles)], atm_adj.at[0], 7)
    high_adj_copy = local(atm_adj_hbm.at[pl.ds(half_tiles, half_tiles)], atm_adj.at[1], 8)
    for copy in small_copies + [weights_copy, field_copy, low_adj_copy]:
        copy.start()

    @pl.when(g == 0)
    def _():
        high_adj_copy.start()

    patient = jnp.logical_and(s == 0, g == 1)
    prompt = jnp.logical_not(patient)

    def meet():
        peers = 1 + has_before.astype(jnp.int32) + 2 * sends_on.astype(jnp.int32)
        pl.semaphore_wait(barrier, peers)

    def partner_field(part):
        return remote(atm_hbm, partner_fields.at[0], 0, s, 1 - part)

    def before_field(part):
        landing = own_fields if part == 1 else partner_fields
        return remote(atm_hbm, landing.at[1], 1 + part, before, 1)

    def before_adjacency():
        return remote(atm_adj_hbm.at[pl.ds(0, half_tiles)], atm_adj.at[1], 3, before, 1)

    def send_fields():
        @pl.when(g == 0)
        def _():
            partner_field(0).start()

            @pl.when(has_before)
            def _():
                before_adjacency().start()

        @pl.when(g == 1)
        def _():
            partner_field(1).start()

            @pl.when(has_before)
            def _():
                before_field(1).start()

    @pl.when(prompt)
    def _():
        meet()
        send_fields()

    for copy in small_copies:
        copy.wait()

    live = count[0]
    upper = 1 - lower_lanes(ROWS).astype(jnp.int32)

    def store_links(links, first, adjacency, number):
        for k in range(number):
            even, odd = block_links(adjacency[k])
            links[first + 2 * k] = even
            links[first + 2 * k + 1] = odd

    def store_places(block_of):
        for t in range(tiles):
            places[t] = jnp.where(t < live, block_of(t), -2) - upper

    def scatter(out, part, number):
        group = 4

        def step(i, carry):
            sums = [jnp.zeros((ROWS, LANES), F32) for _ in range(group)]
            for t in range(tiles):
                place, term = places[t], terms[t]
                for j in range(group):
                    first = 2 * (i * group + j)
                    sums[j] = sums[j] + jnp.where(place == first, term, 0.0)
            for j in range(group):
                out[part, i * group + j] = sums[j]
            return carry

        lax.fori_loop(0, number // group, step, 0)

    def pick_ocean(part):
        def gather(t):
            got[t] = pick_lanes(lambda k: ocean[part, k], ocean_tiles, ocean_links[source[t]])

        each(tiles, GATHER, gather)

        def join(t):
            block = source[t]
            tile = ocean[part, block >> 1]
            field = jnp.where(upper * 0 + (block & 1) == 0, tile, roll_half(tile))
            slope = roll_half(got[t]) - got[t]
            picked[t, : 2 * ROWS] = stacked(jnp.where(lower_lanes(ROWS), field, slope))

        each(tiles, JOIN, join)

    def forward():
        for t in range(tiles):
            product = lax.dot_general(
                picked[t, : 2 * ROWS],
                split_weights[t],
                (((1,), (1,)), ((), ())),
                preferred_element_type=F32,
            )
            added = product[:ROWS] + product[ROWS:]
            terms[t] = added + roll_half(added)

    run_start = g * half_tiles * 2
    store_links(ocean_links, 0, ocean_adj, ocean_tiles)
    store_places(lambda t: target[t] - run_start)
    pick_ocean(1 - g)
    weights_copy.wait()

    def split(t):
        split_weights[t] = stacked(weights[t])

    each(tiles, 4, split)
    forward()
    scatter(partial, 0, atm_tiles)

    low_half, high_half = pl.ds(0, half_tiles), pl.ds(half_tiles, half_tiles)

    def following_sum(part):
        return remote(partial.at[part, high_half], from_behind, 5 + part, following, part)

    def partner_sum(part):
        if part == 0:
            return remote(partial.at[0], from_partner, 4, s, 1)
        return remote(partial.at[0, low_half], from_partner.at[low_half], 4, s, 0)

    def send_partner_columns():
        @pl.when(g == 0)
        def _():
            partner_sum(0).start()

            @pl.when(has_before)
            def _():
                before_field(0).start()

        @pl.when(g == 1)
        def _():
            partner_sum(1).start()

        @pl.when(sends_on)
        def _():
            following_sum(0).start()

    def send_own_columns():
        @pl.when(sends_on)
        def _():
            following_sum(1).start()

    pl.when(prompt)(send_partner_columns)
    pick_ocean(g)
    forward()
    scatter(partial, 1, atm_tiles)
    pl.when(prompt)(send_own_columns)

    is_last = jnp.logical_not(has_following).astype(jnp.int32)

    def pick_atm(fields):
        def place_of(t):
            block = jnp.clip(target[t] - run_start, 0, 2 * atm_tiles - 1)
            past = g * (block >= atm_tiles).astype(jnp.int32)
            return block, past

        def gather(t):
            block, past = place_of(t)
            got[t] = pick_lanes(
                lambda k: fields[past, k], atm_tiles, atm_links[block]
            )

        each(tiles, GATHER, gather)

        def join(t):
            block, past = place_of(t)
            tile = fields[past, (block + run_start - 2 * atm_tiles * past) >> 1]
            turned = roll_half(tile)
            lower = lower_lanes(ROWS)
            keep = upper * 0 + past * is_last == 0
            field = jnp.where(upper == (block & 1), tile, turned)
            ahead = roll_half(got[t]) - got[t]
            slope = jnp.where(lower, -ahead, ahead)
            picked[t, : 2 * ROWS] = stacked(jnp.where(keep, field, 0.0))
            picked[t, 2 * ROWS :] = stacked(jnp.where(keep, slope, 0.0))

        each(tiles, JOIN, join)

    def backward():
        lower = lower_lanes(ROWS)
        for t in range(tiles):
            product = jnp.dot(picked[t], split_weights[t], preferred_element_type=F32)
            field = product[:ROWS] + product[ROWS : 2 * ROWS]
            slope = product[2 * ROWS : 3 * ROWS] + product[3 * ROWS :]
            both = jnp.where(lower, field, slope)
            terms[t] = both + roll_half(both)

    low_adj_copy.wait()
    field_copy.wait()

    @pl.when(g == 0)
    def _():
        high_adj_copy.wait()

    @pl.when(sends_on)
    def _():
        before_adjacency().wait_recv()
        before_field(1).wait_recv()

    store_links(atm_links, 0, atm_adj.at[0], half_tiles)
    store_links(atm_links, 2 * half_tiles, atm_adj.at[1], half_tiles)
    store_places(lambda t: source[t])
    pick_atm(own_fields)
    backward()
    scatter(ocean_out, g, ocean_tiles)

    @pl.when(patient)
    def _():
        meet()
        send_fields()
        send_partner_columns()
        send_own_columns()

    @pl.when(g == 0)
    def _():
        partner_field(1).wait_recv()

    @pl.when(g == 1)
    def _():
        partner_field(0).wait_recv()

    @pl.when(sends_on)
    def _():
        before_field(0).wait_recv()

    pick_atm(partner_fields)
    backward()
    scatter(ocean_out, 1 - g, ocean_tiles)

    def behind_sum():
        return jnp.where(has_before, from_behind[...], 0.0)

    @pl.when(g == 0)
    def _():
        partner_sum(1).wait_recv()

        @pl.when(has_before)
        def _():
            following_sum(0).wait_recv()

        atm_out[low_half] = partial[1, low_half] + behind_sum()
        atm_out[high_half] = partial[1, high_half] + from_partner[low_half]

    @pl.when(g == 1)
    def _():
        partner_sum(0).wait_recv()

        @pl.when(has_before)
        def _():
            following_sum(1).wait_recv()

        atm_out[low_half] = from_partner[low_half] + behind_sum()
        atm_out[high_half] = from_partner[high_half] + partial[1, low_half]

    @pl.when(g == 0)
    def _():
        partner_field(0).wait_send()
        partner_sum(0).wait_send()

        @pl.when(has_before)
        def _():
            before_adjacency().wait_send()
            before_field(0).wait_send()

    @pl.when(g == 1)
    def _():
        partner_field(1).wait_send()
        partner_sum(1).wait_send()

        @pl.when(has_before)
        def _():
            before_field(1).wait_send()

    @pl.when(sends_on)
    def _():
        following_sum(0).wait_send()
        following_sum(1).wait_send()


def as_tiles(x):
    rows, cells = x.shape
    return x.reshape(rows, cells // LANES, LANES).transpose(1, 0, 2)


def write_kernel(atm, ocean, atm_out, ocean_out, sem):
    copies = [
        pltpu.make_async_copy(atm, atm_out, sem.at[0]),
        pltpu.make_async_copy(ocean, ocean_out, sem.at[1]),
    ]
    for copy in copies:
        copy.start()
    for copy in copies:
        copy.wait()


def write_out(atm, ocean):
    return pl.pallas_call(
        write_kernel,
        out_shape=(
            jax.ShapeDtypeStruct(atm.shape, F32),
            jax.ShapeDtypeStruct(ocean.shape, F32),
        ),
        in_specs=[pl.BlockSpec(memory_space=pltpu.VMEM)] * 2,
        out_specs=[pl.BlockSpec(memory_space=pltpu.HBM)] * 2,
        scratch_shapes=[pltpu.SemaphoreType.DMA((2,))],
    )(
        pltpu.with_memory_space_constraint(atm, pltpu.VMEM),
        pltpu.with_memory_space_constraint(ocean, pltpu.VMEM),
    )


def per_device(
    n_sfc,
    ocean_field,
    atm_field,
    tile_weights,
    tile_source,
    tile_target,
    tile_count,
    ocean_adjacency,
    atm_adjacency,
):
    columns, ocean_cells = ocean_field.shape
    half_columns, atm_cells = atm_field.shape
    tiles = tile_source.shape[0]
    ocean_tiles = ocean_cells // LANES
    atm_tiles = atm_cells // LANES
    half_tiles = atm_tiles // 2
    vmem = pl.BlockSpec(memory_space=pltpu.VMEM)
    atm_out, ocean_out = pl.pallas_call(
        functools.partial(kernel, n_sfc),
        out_shape=(
            pltpu.VMEM((atm_tiles, ROWS, LANES), F32),
            pltpu.VMEM((2, ocean_tiles, ROWS, LANES), F32),
        ),
        in_specs=[pl.BlockSpec(memory_space=pltpu.HBM)] * 8,
        out_specs=(vmem, vmem),
        scratch_shapes=[
            pltpu.VMEM((2, ocean_tiles, ROWS, LANES), F32),
            pltpu.VMEM((2, atm_tiles, ROWS, LANES), F32),
            pltpu.VMEM((2, atm_tiles, ROWS, LANES), F32),
            pltpu.VMEM((ocean_tiles, 2, LANES), jnp.int32),
            pltpu.VMEM((2, half_tiles, 2, LANES), jnp.int32),
            pltpu.VMEM(tile_weights.shape, F32),
            pltpu.SMEM((tiles,), jnp.int32),
            pltpu.SMEM((tiles,), jnp.int32),
            pltpu.SMEM((1,), jnp.int32),
            pltpu.VMEM((2 * ocean_tiles, ROWS, LANES), jnp.int32),
            pltpu.VMEM((2 * atm_tiles, ROWS, LANES), jnp.int32),
            pltpu.VMEM((tiles, 2 * TB, LANES), BF16),
            pltpu.VMEM((tiles, ROWS, LANES), F32),
            pltpu.VMEM((tiles, 4 * ROWS, LANES), BF16),
            pltpu.VMEM((tiles, ROWS, LANES), F32),
            pltpu.VMEM((tiles, ROWS, LANES), jnp.int32),
            pltpu.VMEM((2, atm_tiles, ROWS, LANES), F32),
            pltpu.VMEM((atm_tiles, ROWS, LANES), F32),
            pltpu.VMEM((half_tiles, ROWS, LANES), F32),
            pltpu.SemaphoreType.DMA((9,)),
            pltpu.SemaphoreType.DMA((7,)),
            pltpu.SemaphoreType.DMA((7,)),
        ],
        compiler_params=pltpu.CompilerParams(
            collective_id=0, has_side_effects=True, vmem_limit_bytes=VLIM
        ),
    )(
        ocean_field.reshape(2, ROWS, ocean_tiles, LANES).transpose(0, 2, 1, 3),
        as_tiles(atm_field),
        tile_weights,
        tile_source,
        tile_target,
        tile_count,
        as_tiles(ocean_adjacency),
        as_tiles(atm_adjacency),
    )
    atm_out, ocean_out = write_out(atm_out, ocean_out)
    return (
        atm_out.transpose(1, 0, 2).reshape(half_columns, atm_cells),
        ocean_out.transpose(0, 2, 1, 3).reshape(columns, ocean_cells),
    )


def solution(mesh):
    return jax.shard_map(
        functools.partial(per_device, mesh.shape["sfc"]),
        mesh=mesh,
        in_specs=(
            P(None, ("sfc", "grp")),
            P("grp", "sfc"),
            P(("sfc", "grp"), None, None),
            P(("sfc", "grp")),
            P(("sfc", "grp")),
            P(("sfc", "grp")),
            P(None, ("sfc", "grp")),
            P(None, "sfc"),
        ),
        out_specs=(P("grp", "sfc"), P(None, ("sfc", "grp"))),
        check_vma=False,
    )
```

```python
import functools

import jax
import jax.numpy as jnp
from jax import lax
from jax.experimental import pallas as pl
from jax.experimental.pallas import tpu as pltpu
from jax.sharding import PartitionSpec as P

TB = 64
LANES = 128
ROWS = 8
GATHER = 24
JOIN = 24
VLIM = 63 * 1024 * 1024
MESH = pl.DeviceIdType.MESH
F32 = jnp.float32
BF16 = jnp.bfloat16


def roll_half(x):
    return pltpu.roll(x, TB, x.ndim - 1)


def lower_lanes(rows):
    return lax.broadcasted_iota(jnp.int32, (rows, LANES), 1) < TB


def pick_lanes(load, count, index):
    low = index & (LANES - 1)
    high = index >> 7
    bits = [(high >> b) & 1 == 1 for b in range((count - 1).bit_length())]

    def tree(first, level):
        if level < 0:
            return jnp.take_along_axis(load(first), low, axis=1, mode="promise_in_bounds")
        left = tree(first, level - 1)
        right = tree(first + (1 << level), level - 1)
        return jnp.where(bits[level], right, left)

    return tree(0, len(bits) - 1)


def stacked(x):
    high = x.astype(BF16).astype(F32)
    return jnp.concatenate([high, x - high], axis=0).astype(BF16)


def block_links(links):
    ahead = jnp.broadcast_to(links[1:2], (ROWS, LANES))
    behind = jnp.broadcast_to(links[0:1], (ROWS, LANES))
    lower = lower_lanes(ROWS)
    return (
        jnp.where(lower, ahead, roll_half(behind)),
        jnp.where(lower, roll_half(ahead), behind),
    )


def each(count, group, body):
    def step(i, carry):
        for j in range(group):
            body(i * group + j)
        return carry

    if group == count:
        step(0, 0)
    else:
        lax.fori_loop(0, count // group, step, 0)


def kernel(
    n_sfc,
    ocean_hbm,
    atm_hbm,
    weights_hbm,
    source_hbm,
    target_hbm,
    count_hbm,
    ocean_adj_hbm,
    atm_adj_hbm,
    atm_out,
    ocean_out,
    ocean,
    own_fields,
    partner_fields,
    ocean_adj,
    atm_adj,
    weights,
    source,
    target,
    count,
    ocean_links,
    atm_links,
    split_weights,
    got,
    picked,
    terms,
    places,
    partial,
    from_partner,
    from_behind,
    local_sem,
    send_sem,
    recv_sem,
):
    s = lax.axis_index("sfc")
    g = lax.axis_index("grp")
    ocean_tiles = ocean.shape[1]
    atm_tiles = atm_hbm.shape[0]
    half_tiles = atm_tiles // 2
    tiles = weights.shape[0]
    has_following = s < n_sfc - 1
    has_before = s > 0
    following = jnp.minimum(s + 1, n_sfc - 1)
    before = jnp.maximum(s - 1, 0)
    sends_on = jnp.logical_and(g == 1, has_following)

    def local(src, dst, number):
        return pltpu.make_async_copy(src, dst, local_sem.at[number])

    def remote(src, dst, number, sfc, grp):
        return pltpu.make_async_remote_copy(
            src_ref=src,
            dst_ref=dst,
            send_sem=send_sem.at[number],
            recv_sem=recv_sem.at[number],
            device_id={"sfc": sfc, "grp": grp},
            device_id_type=MESH,
        )

    barrier = pltpu.get_barrier_semaphore()

    def greet(sfc, grp):
        pl.semaphore_signal(
            barrier, inc=1, device_id={"sfc": sfc, "grp": grp}, device_id_type=MESH
        )

    greet(s, 1 - g)

    @pl.when(has_before)
    def _():
        greet(before, 1)

    @pl.when(sends_on)
    def _():
        greet(following, 0)
        greet(following, 1)

    small_copies = [
        local(source_hbm, source, 0),
        local(target_hbm, target, 1),
        local(count_hbm, count, 2),
        local(ocean_adj_hbm, ocean_adj, 3),
        local(ocean_hbm, ocean, 4),
    ]
    weights_copy = local(weights_hbm, weights, 5)
    field_copy = local(atm_hbm, own_fields.at[0], 6)
    low_adj_copy = local(atm_adj_hbm.at[pl.ds(g * half_tiles, half_tiles)], atm_adj.at[0], 7)
    high_adj_copy = local(atm_adj_hbm.at[pl.ds(half_tiles, half_tiles)], atm_adj.at[1], 8)
    for copy in small_copies + [weights_copy, field_copy, low_adj_copy]:
        copy.start()

    @pl.when(g == 0)
    def _():
        high_adj_copy.start()

    patient = jnp.logical_and(s == 0, g == 1)
    prompt = jnp.logical_not(patient)

    def meet():
        peers = 1 + has_before.astype(jnp.int32) + 2 * sends_on.astype(jnp.int32)
        pl.semaphore_wait(barrier, peers)

    def partner_field(part):
        return remote(atm_hbm, partner_fields.at[0], 0, s, 1 - part)

    def before_field(part):
        landing = own_fields if part == 1 else partner_fields
        return remote(atm_hbm, landing.at[1], 1 + part, before, 1)

    def before_adjacency():
        return remote(atm_adj_hbm.at[pl.ds(0, half_tiles)], atm_adj.at[1], 3, before, 1)

    def send_fields():
        @pl.when(g == 0)
        def _():
            partner_field(0).start()

            @pl.when(has_before)
            def _():
                before_adjacency().start()

        @pl.when(g == 1)
        def _():
            partner_field(1).start()

            @pl.when(has_before)
            def _():
                before_field(1).start()

    @pl.when(prompt)
    def _():
        meet()
        send_fields()

    for copy in small_copies:
        copy.wait()

    live = count[0]
    upper = 1 - lower_lanes(ROWS).astype(jnp.int32)

    def store_links(links, first, adjacency, number):
        for k in range(number):
            even, odd = block_links(adjacency[k])
            links[first + 2 * k] = even
            links[first + 2 * k + 1] = odd

    def store_places(block_of):
        for t in range(tiles):
            places[t] = jnp.where(t < live, block_of(t), -2) - upper

    def scatter(out, part, first_tile, number):
        group = 4

        def step(i, carry):
            sums = [jnp.zeros((ROWS, LANES), F32) for _ in range(group)]
            for t in range(tiles):
                place, term = places[t], terms[t]
                for j in range(group):
                    first = 2 * (first_tile + i * group + j)
                    sums[j] = sums[j] + jnp.where(place == first, term, 0.0)
            for j in range(group):
                out[part, first_tile + i * group + j] = sums[j]
            return carry

        lax.fori_loop(0, number // group, step, 0)

    def pick_ocean(part, group):
        for t in group:
            got[t] = pick_lanes(lambda k: ocean[part, k], ocean_tiles, ocean_links[source[t]])

        for t in group:
            block = source[t]
            tile = ocean[part, block >> 1]
            field = jnp.where(upper * 0 + (block & 1) == 0, tile, roll_half(tile))
            slope = roll_half(got[t]) - got[t]
            picked[t, : 2 * ROWS] = stacked(jnp.where(lower_lanes(ROWS), field, slope))

    def forward(group):
        for t in group:
            product = lax.dot_general(
                picked[t, : 2 * ROWS],
                split_weights[t],
                (((1,), (1,)), ((), ())),
                preferred_element_type=F32,
            )
            added = product[:ROWS] + product[ROWS:]
            terms[t] = added + roll_half(added)

    run_start = g * half_tiles * 2
    store_links(ocean_links, 0, ocean_adj, ocean_tiles)
    store_places(lambda t: target[t] - run_start)
    weights_copy.wait()
    group_size = 24
    groups = [range(i, i + group_size) for i in range(0, tiles, group_size)]
    for group in groups:
        pick_ocean(1 - g, group)
        for t in group:
            split_weights[t] = stacked(weights[t])
        forward(group)
    scatter(partial, 0, 0, half_tiles)

    low_half, high_half = pl.ds(0, half_tiles), pl.ds(half_tiles, half_tiles)

    def following_sum(part):
        return remote(partial.at[part, high_half], from_behind, 5 + part, following, part)

    def partner_low(part):
        return remote(partial.at[0, low_half], from_partner.at[low_half], 4, s, 1 - part)

    def partner_high():
        return remote(partial.at[0, high_half], from_partner.at[high_half], 7, s, 1)

    def send_low():
        for part in range(2):
            pl.when(g == part)(partner_low(part).start)

    pl.when(prompt)(send_low)
    scatter(partial, 0, half_tiles, half_tiles)

    def send_high():
        @pl.when(g == 0)
        def _():
            partner_high().start()

            @pl.when(has_before)
            def _():
                before_field(0).start()

        @pl.when(sends_on)
        def _():
            following_sum(0).start()

    def send_own_columns():
        @pl.when(sends_on)
        def _():
            following_sum(1).start()

    pl.when(prompt)(send_high)
    for group in groups:
        pick_ocean(g, group)
        forward(group)
    scatter(partial, 1, 0, atm_tiles)
    pl.when(prompt)(send_own_columns)

    is_last = jnp.logical_not(has_following).astype(jnp.int32)

    def pick_atm(fields):
        def place_of(t):
            block = jnp.clip(target[t] - run_start, 0, 2 * atm_tiles - 1)
            past = g * (block >= atm_tiles).astype(jnp.int32)
            return block, past

        def gather(t):
            block, past = place_of(t)
            got[t] = pick_lanes(
                lambda k: fields[past, k], atm_tiles, atm_links[block]
            )

        each(tiles, GATHER, gather)

        def join(t):
            block, past = place_of(t)
            tile = fields[past, (block + run_start - 2 * atm_tiles * past) >> 1]
            turned = roll_half(tile)
            lower = lower_lanes(ROWS)
            keep = upper * 0 + past * is_last == 0
            field = jnp.where(upper == (block & 1), tile, turned)
            ahead = roll_half(got[t]) - got[t]
            slope = jnp.where(lower, -ahead, ahead)
            picked[t, : 2 * ROWS] = stacked(jnp.where(keep, field, 0.0))
            picked[t, 2 * ROWS :] = stacked(jnp.where(keep, slope, 0.0))

        each(tiles, JOIN, join)

    def backward():
        lower = lower_lanes(ROWS)
        for t in range(tiles):
            product = jnp.dot(picked[t], split_weights[t], preferred_element_type=F32)
            field = product[:ROWS] + product[ROWS : 2 * ROWS]
            slope = product[2 * ROWS : 3 * ROWS] + product[3 * ROWS :]
            both = jnp.where(lower, field, slope)
            terms[t] = both + roll_half(both)

    low_adj_copy.wait()
    field_copy.wait()

    @pl.when(g == 0)
    def _():
        high_adj_copy.wait()

    @pl.when(sends_on)
    def _():
        before_adjacency().wait_recv()
        before_field(1).wait_recv()

    store_links(atm_links, 0, atm_adj.at[0], half_tiles)
    store_links(atm_links, 2 * half_tiles, atm_adj.at[1], half_tiles)
    store_places(lambda t: source[t])
    pick_atm(own_fields)
    backward()
    scatter(ocean_out, g, 0, ocean_tiles)

    @pl.when(patient)
    def _():
        meet()
        send_fields()
        send_low()
        send_high()
        send_own_columns()

    @pl.when(g == 0)
    def _():
        partner_field(1).wait_recv()

    @pl.when(g == 1)
    def _():
        partner_field(0).wait_recv()

    @pl.when(sends_on)
    def _():
        before_field(0).wait_recv()

    pick_atm(partner_fields)
    backward()
    scatter(ocean_out, 1 - g, 0, ocean_tiles)

    def behind_sum():
        return jnp.where(has_before, from_behind[...], 0.0)

    @pl.when(g == 0)
    def _():
        partner_low(1).wait_recv()

        @pl.when(has_before)
        def _():
            following_sum(0).wait_recv()

        atm_out[low_half] = partial[1, low_half] + behind_sum()
        atm_out[high_half] = partial[1, high_half] + from_partner[low_half]

    @pl.when(g == 1)
    def _():
        partner_low(0).wait_recv()

        @pl.when(has_before)
        def _():
            following_sum(1).wait_recv()

        atm_out[low_half] = from_partner[low_half] + behind_sum()
        partner_high().wait_recv()
        atm_out[high_half] = from_partner[high_half] + partial[1, low_half]

    @pl.when(g == 0)
    def _():
        partner_field(0).wait_send()
        partner_low(0).wait_send()
        partner_high().wait_send()

        @pl.when(has_before)
        def _():
            before_adjacency().wait_send()
            before_field(0).wait_send()

    @pl.when(g == 1)
    def _():
        partner_field(1).wait_send()
        partner_low(1).wait_send()

        @pl.when(has_before)
        def _():
            before_field(1).wait_send()

    @pl.when(sends_on)
    def _():
        following_sum(0).wait_send()
        following_sum(1).wait_send()


def as_tiles(x):
    rows, cells = x.shape
    return x.reshape(rows, cells // LANES, LANES).transpose(1, 0, 2)


def write_kernel(atm, ocean, atm_out, ocean_out, sem):
    copies = [
        pltpu.make_async_copy(atm, atm_out, sem.at[0]),
        pltpu.make_async_copy(ocean, ocean_out, sem.at[1]),
    ]
    for copy in copies:
        copy.start()
    for copy in copies:
        copy.wait()


def write_out(atm, ocean):
    return pl.pallas_call(
        write_kernel,
        out_shape=(
            jax.ShapeDtypeStruct(atm.shape, F32),
            jax.ShapeDtypeStruct(ocean.shape, F32),
        ),
        in_specs=[pl.BlockSpec(memory_space=pltpu.VMEM)] * 2,
        out_specs=[pl.BlockSpec(memory_space=pltpu.HBM)] * 2,
        scratch_shapes=[pltpu.SemaphoreType.DMA((2,))],
    )(
        pltpu.with_memory_space_constraint(atm, pltpu.VMEM),
        pltpu.with_memory_space_constraint(ocean, pltpu.VMEM),
    )


def per_device(
    n_sfc,
    ocean_field,
    atm_field,
    tile_weights,
    tile_source,
    tile_target,
    tile_count,
    ocean_adjacency,
    atm_adjacency,
):
    columns, ocean_cells = ocean_field.shape
    half_columns, atm_cells = atm_field.shape
    tiles = tile_source.shape[0]
    ocean_tiles = ocean_cells // LANES
    atm_tiles = atm_cells // LANES
    half_tiles = atm_tiles // 2
    vmem = pl.BlockSpec(memory_space=pltpu.VMEM)
    atm_out, ocean_out = pl.pallas_call(
        functools.partial(kernel, n_sfc),
        out_shape=(
            pltpu.VMEM((atm_tiles, ROWS, LANES), F32),
            pltpu.VMEM((2, ocean_tiles, ROWS, LANES), F32),
        ),
        in_specs=[pl.BlockSpec(memory_space=pltpu.HBM)] * 8,
        out_specs=(vmem, vmem),
        scratch_shapes=[
            pltpu.VMEM((2, ocean_tiles, ROWS, LANES), F32),
            pltpu.VMEM((2, atm_tiles, ROWS, LANES), F32),
            pltpu.VMEM((2, atm_tiles, ROWS, LANES), F32),
            pltpu.VMEM((ocean_tiles, 2, LANES), jnp.int32),
            pltpu.VMEM((2, half_tiles, 2, LANES), jnp.int32),
            pltpu.VMEM(tile_weights.shape, F32),
            pltpu.SMEM((tiles,), jnp.int32),
            pltpu.SMEM((tiles,), jnp.int32),
            pltpu.SMEM((1,), jnp.int32),
            pltpu.VMEM((2 * ocean_tiles, ROWS, LANES), jnp.int32),
            pltpu.VMEM((2 * atm_tiles, ROWS, LANES), jnp.int32),
            pltpu.VMEM((tiles, 2 * TB, LANES), BF16),
            pltpu.VMEM((tiles, ROWS, LANES), F32),
            pltpu.VMEM((tiles, 4 * ROWS, LANES), BF16),
            pltpu.VMEM((tiles, ROWS, LANES), F32),
            pltpu.VMEM((tiles, ROWS, LANES), jnp.int32),
            pltpu.VMEM((2, atm_tiles, ROWS, LANES), F32),
            pltpu.VMEM((atm_tiles, ROWS, LANES), F32),
            pltpu.VMEM((half_tiles, ROWS, LANES), F32),
            pltpu.SemaphoreType.DMA((9,)),
            pltpu.SemaphoreType.DMA((8,)),
            pltpu.SemaphoreType.DMA((8,)),
        ],
        compiler_params=pltpu.CompilerParams(
            collective_id=0, has_side_effects=True, vmem_limit_bytes=VLIM
        ),
    )(
        ocean_field.reshape(2, ROWS, ocean_tiles, LANES).transpose(0, 2, 1, 3),
        as_tiles(atm_field),
        tile_weights,
        tile_source,
        tile_target,
        tile_count,
        as_tiles(ocean_adjacency),
        as_tiles(atm_adjacency),
    )
    atm_out, ocean_out = write_out(atm_out, ocean_out)
    return (
        atm_out.transpose(1, 0, 2).reshape(half_columns, atm_cells),
        ocean_out.transpose(0, 2, 1, 3).reshape(columns, ocean_cells),
    )


def solution(mesh):
    return jax.shard_map(
        functools.partial(per_device, mesh.shape["sfc"]),
        mesh=mesh,
        in_specs=(
            P(None, ("sfc", "grp")),
            P("grp", "sfc"),
            P(("sfc", "grp"), None, None),
            P(("sfc", "grp")),
            P(("sfc", "grp")),
            P(("sfc", "grp")),
            P(None, ("sfc", "grp")),
            P(None, "sfc"),
        ),
        out_specs=(P("grp", "sfc"), P(None, ("sfc", "grp"))),
        check_vma=False,
    )
```

```python
import functools

import jax
import jax.numpy as jnp
from jax import lax
from jax.experimental import pallas as pl
from jax.experimental.pallas import tpu as pltpu
from jax.sharding import PartitionSpec as P

TB = 64
LANES = 128
ROWS = 8
GATHER = 24
JOIN = 24
VLIM = 63 * 1024 * 1024
MESH = pl.DeviceIdType.MESH
F32 = jnp.float32
BF16 = jnp.bfloat16


def roll_half(x):
    return pltpu.roll(x, TB, x.ndim - 1)


def lower_lanes(rows):
    return lax.broadcasted_iota(jnp.int32, (rows, LANES), 1) < TB


def pick_lanes(load, count, index):
    low = index & (LANES - 1)
    high = index >> 7
    bits = [(high >> b) & 1 == 1 for b in range((count - 1).bit_length())]

    def tree(first, level):
        if level < 0:
            return jnp.take_along_axis(load(first), low, axis=1, mode="promise_in_bounds")
        left = tree(first, level - 1)
        right = tree(first + (1 << level), level - 1)
        return jnp.where(bits[level], right, left)

    return tree(0, len(bits) - 1)


def stacked(x):
    high = x.astype(BF16).astype(F32)
    return jnp.concatenate([high, x - high], axis=0).astype(BF16)


def block_links(links):
    ahead = jnp.broadcast_to(links[1:2], (ROWS, LANES))
    behind = jnp.broadcast_to(links[0:1], (ROWS, LANES))
    lower = lower_lanes(ROWS)
    return (
        jnp.where(lower, ahead, roll_half(behind)),
        jnp.where(lower, roll_half(ahead), behind),
    )


def each(count, group, body):
    def step(i, carry):
        for j in range(group):
            body(i * group + j)
        return carry

    if group == count:
        step(0, 0)
    else:
        lax.fori_loop(0, count // group, step, 0)


def kernel(
    n_sfc,
    ocean_hbm,
    atm_hbm,
    weights_hbm,
    source_hbm,
    target_hbm,
    count_hbm,
    ocean_adj_hbm,
    atm_adj_hbm,
    atm_out,
    ocean_out,
    partner_ocean,
    own_ocean,
    own_fields,
    partner_fields,
    ocean_adj,
    atm_adj,
    weights,
    source,
    target,
    count,
    ocean_links,
    atm_links,
    split_weights,
    got,
    picked,
    terms,
    places,
    partial,
    from_partner,
    from_behind,
    local_sem,
    send_sem,
    recv_sem,
):
    s = lax.axis_index("sfc")
    g = lax.axis_index("grp")
    ocean_tiles = own_ocean.shape[0]
    atm_tiles = atm_hbm.shape[0]
    half_tiles = atm_tiles // 2
    tiles = weights.shape[0]
    has_following = s < n_sfc - 1
    has_before = s > 0
    following = jnp.minimum(s + 1, n_sfc - 1)
    before = jnp.maximum(s - 1, 0)
    sends_on = jnp.logical_and(g == 1, has_following)

    def local(src, dst, number):
        return pltpu.make_async_copy(src, dst, local_sem.at[number])

    def remote(src, dst, number, sfc, grp):
        return pltpu.make_async_remote_copy(
            src_ref=src,
            dst_ref=dst,
            send_sem=send_sem.at[number],
            recv_sem=recv_sem.at[number],
            device_id={"sfc": sfc, "grp": grp},
            device_id_type=MESH,
        )

    barrier = pltpu.get_barrier_semaphore()

    def greet(sfc, grp):
        pl.semaphore_signal(
            barrier, inc=1, device_id={"sfc": sfc, "grp": grp}, device_id_type=MESH
        )

    first = s == 0
    unmet = jnp.logical_and(first, g == 1)

    @pl.when(jnp.logical_not(jnp.logical_and(first, g == 0)))
    def _():
        greet(s, 1 - g)

    @pl.when(has_before)
    def _():
        greet(before, 1)

    @pl.when(sends_on)
    def _():
        greet(following, 0)
        greet(following, 1)

    small_copies = [
        local(source_hbm, source, 0),
        local(target_hbm, target, 1),
        local(count_hbm, count, 2),
        local(ocean_adj_hbm, ocean_adj, 3),
        local(ocean_hbm.at[1 - g], partner_ocean, 4),
    ]
    ocean_copy = local(ocean_hbm.at[g], own_ocean, 9)
    weights_copy = local(weights_hbm, weights, 5)
    field_copy = local(atm_hbm, own_fields.at[0], 6)
    low_adj_copy = local(atm_adj_hbm.at[pl.ds(g * half_tiles, half_tiles)], atm_adj.at[0], 7)
    high_adj_copy = local(atm_adj_hbm.at[pl.ds(half_tiles, half_tiles)], atm_adj.at[1], 8)
    for copy in small_copies + [weights_copy]:
        copy.start()

    peers = 1 - unmet.astype(jnp.int32) + has_before.astype(jnp.int32)
    pl.semaphore_wait(barrier, peers + 2 * sends_on.astype(jnp.int32))

    def partner_field(part):
        return remote(atm_hbm, partner_fields.at[0], 0, s, 1 - part)

    def before_field(part):
        landing = own_fields if part == 1 else partner_fields
        return remote(atm_hbm, landing.at[1], 1 + part, before, 1)

    def before_adjacency():
        return remote(atm_adj_hbm.at[pl.ds(0, half_tiles)], atm_adj.at[1], 3, before, 1)

    @pl.when(g == 0)
    def _():
        partner_field(0).start()

        @pl.when(has_before)
        def _():
            before_adjacency().start()

    @pl.when(g == 1)
    def _():
        @pl.when(has_before)
        def _():
            before_field(1).start()
            partner_field(1).start()

    for copy in [ocean_copy, field_copy, low_adj_copy]:
        copy.start()

    @pl.when(g == 0)
    def _():
        high_adj_copy.start()

    for copy in small_copies:
        copy.wait()

    live = count[0]
    upper = 1 - lower_lanes(ROWS).astype(jnp.int32)

    def store_links(links, first, adjacency, number):
        for k in range(number):
            even, odd = block_links(adjacency[k])
            links[first + 2 * k] = even
            links[first + 2 * k + 1] = odd

    def store_places(block_of):
        for t in range(tiles):
            places[t] = jnp.where(t < live, block_of(t), -2) - upper

    def scatter(out, part, first_tile, number):
        group = 16

        def step(i, carry):
            sums = [jnp.zeros((ROWS, LANES), F32) for _ in range(group)]
            for t in range(tiles):
                place, term = places[t], terms[t]
                for j in range(group):
                    first = 2 * (first_tile + i * group + j)
                    sums[j] = sums[j] + jnp.where(place == first, term, 0.0)
            for j in range(group):
                out[part, first_tile + i * group + j] = sums[j]
            return carry

        lax.fori_loop(0, number // group, step, 0)

    def pick_ocean(ocean, group):
        for t in group:
            got[t] = pick_lanes(lambda k: ocean[k], ocean_tiles, ocean_links[source[t]])

        for t in group:
            block = source[t]
            tile = ocean[block >> 1]
            field = jnp.where(upper * 0 + (block & 1) == 0, tile, roll_half(tile))
            slope = roll_half(got[t]) - got[t]
            picked[t, : 2 * ROWS] = stacked(jnp.where(lower_lanes(ROWS), field, slope))

    def forward(group):
        for t in group[::2]:
            product = lax.dot_general(
                jnp.concatenate([picked[t, : 2 * ROWS], picked[t + 1, : 2 * ROWS]], axis=0),
                jnp.concatenate([split_weights[t], split_weights[t + 1]], axis=0),
                (((1,), (1,)), ((), ())),
                preferred_element_type=F32,
            )
            for j in range(2):
                mine = product[2 * ROWS * j : 2 * ROWS * (j + 1), LANES * j : LANES * (j + 1)]
                added = mine[:ROWS] + mine[ROWS:]
                terms[t + j] = added + roll_half(added)

    run_start = g * half_tiles * 2
    store_links(ocean_links, 0, ocean_adj, ocean_tiles)
    group_size = 24
    groups = [range(i, i + group_size) for i in range(0, tiles, group_size)]
    for group in groups:
        pick_ocean(partner_ocean, group)
        weights_copy.wait()
        for t in group:
            split_weights[t] = stacked(weights[t])
        forward(group)
    store_places(lambda t: target[t] - run_start)
    scatter(partial, 0, 0, half_tiles)

    low_half, high_half = pl.ds(0, half_tiles), pl.ds(half_tiles, half_tiles)

    def following_sum(part):
        return remote(partial.at[part, high_half], from_behind, 5 + part, following, part)

    def partner_low(part):
        return remote(partial.at[0, low_half], from_partner.at[low_half], 4, s, 1 - part)

    def partner_high():
        return remote(partial.at[0, high_half], from_partner.at[high_half], 7, s, 1)

    @pl.when(g == 0)
    def _():
        partner_low(0).start()

    @pl.when(jnp.logical_and(g == 1, has_before))
    def _():
        partner_low(1).start()

    scatter(partial, 0, half_tiles, half_tiles)

    @pl.when(g == 0)
    def _():
        partner_high().start()

        @pl.when(has_before)
        def _():
            before_field(0).start()

    @pl.when(sends_on)
    def _():
        following_sum(0).start()

    ocean_copy.wait()
    for group in groups:
        pick_ocean(own_ocean, group)
        forward(group)
    scatter(partial, 1, 0, atm_tiles)

    @pl.when(sends_on)
    def _():
        following_sum(1).start()

    is_last = jnp.logical_not(has_following).astype(jnp.int32)

    def pick_atm(fields):
        def place_of(t):
            block = jnp.clip(target[t] - run_start, 0, 2 * atm_tiles - 1)
            past = g * (block >= atm_tiles).astype(jnp.int32)
            return block, past

        def gather(t):
            block, past = place_of(t)
            got[t] = pick_lanes(
                lambda k: fields[past, k], atm_tiles, atm_links[block]
            )

        each(tiles, GATHER, gather)

        def join(t):
            block, past = place_of(t)
            tile = fields[past, (block + run_start - 2 * atm_tiles * past) >> 1]
            turned = roll_half(tile)
            lower = lower_lanes(ROWS)
            keep = upper * 0 + past * is_last == 0
            field = jnp.where(upper == (block & 1), tile, turned)
            ahead = roll_half(got[t]) - got[t]
            slope = jnp.where(lower, -ahead, ahead)
            picked[t, : 2 * ROWS] = stacked(jnp.where(keep, field, 0.0))
            picked[t, 2 * ROWS :] = stacked(jnp.where(keep, slope, 0.0))

        each(tiles, JOIN, join)

    def backward():
        lower = lower_lanes(ROWS)
        for t in range(tiles):
            product = jnp.dot(picked[t], split_weights[t], preferred_element_type=F32)
            field = product[:ROWS] + product[ROWS : 2 * ROWS]
            slope = product[2 * ROWS : 3 * ROWS] + product[3 * ROWS :]
            both = jnp.where(lower, field, slope)
            terms[t] = both + roll_half(both)

    low_adj_copy.wait()
    field_copy.wait()

    @pl.when(g == 0)
    def _():
        high_adj_copy.wait()

    @pl.when(sends_on)
    def _():
        before_adjacency().wait_recv()
        before_field(1).wait_recv()

    store_links(atm_links, 0, atm_adj.at[0], half_tiles)
    store_links(atm_links, 2 * half_tiles, atm_adj.at[1], half_tiles)
    store_places(lambda t: source[t])
    pick_atm(own_fields)
    backward()
    scatter(ocean_out, g, 0, ocean_tiles)

    @pl.when(g == 0)
    def _():
        partner_field(1).wait_recv()

    @pl.when(g == 1)
    def _():
        partner_field(0).wait_recv()

        @pl.when(first)
        def _():
            partner_field(1).start()
            partner_low(1).start()

    @pl.when(sends_on)
    def _():
        before_field(0).wait_recv()

    pick_atm(partner_fields)
    backward()
    scatter(ocean_out, 1 - g, 0, ocean_tiles)

    def behind_sum():
        return jnp.where(has_before, from_behind[...], 0.0)

    @pl.when(g == 0)
    def _():
        partner_low(1).wait_recv()

        @pl.when(has_before)
        def _():
            following_sum(0).wait_recv()

        atm_out[low_half] = partial[1, low_half] + behind_sum()
        atm_out[high_half] = partial[1, high_half] + from_partner[low_half]

    @pl.when(g == 1)
    def _():
        partner_low(0).wait_recv()

        @pl.when(has_before)
        def _():
            following_sum(1).wait_recv()

        atm_out[low_half] = from_partner[low_half] + behind_sum()
        partner_high().wait_recv()
        atm_out[high_half] = from_partner[high_half] + partial[1, low_half]

    @pl.when(g == 0)
    def _():
        partner_field(0).wait_send()
        partner_low(0).wait_send()
        partner_high().wait_send()

        @pl.when(has_before)
        def _():
            before_adjacency().wait_send()
            before_field(0).wait_send()

    @pl.when(g == 1)
    def _():
        partner_field(1).wait_send()
        partner_low(1).wait_send()

        @pl.when(has_before)
        def _():
            before_field(1).wait_send()

    @pl.when(sends_on)
    def _():
        following_sum(0).wait_send()
        following_sum(1).wait_send()


def as_tiles(x):
    rows, cells = x.shape
    return x.reshape(rows, cells // LANES, LANES).transpose(1, 0, 2)


def write_kernel(atm, ocean, atm_out, ocean_out, sem):
    copies = [
        pltpu.make_async_copy(atm, atm_out, sem.at[0]),
        pltpu.make_async_copy(ocean, ocean_out, sem.at[1]),
    ]
    for copy in copies:
        copy.start()
    for copy in copies:
        copy.wait()


def write_out(atm, ocean):
    return pl.pallas_call(
        write_kernel,
        out_shape=(
            jax.ShapeDtypeStruct(atm.shape, F32),
            jax.ShapeDtypeStruct(ocean.shape, F32),
        ),
        in_specs=[pl.BlockSpec(memory_space=pltpu.VMEM)] * 2,
        out_specs=[pl.BlockSpec(memory_space=pltpu.HBM)] * 2,
        scratch_shapes=[pltpu.SemaphoreType.DMA((2,))],
    )(
        pltpu.with_memory_space_constraint(atm, pltpu.VMEM),
        pltpu.with_memory_space_constraint(ocean, pltpu.VMEM),
    )


def per_device(
    n_sfc,
    ocean_field,
    atm_field,
    tile_weights,
    tile_source,
    tile_target,
    tile_count,
    ocean_adjacency,
    atm_adjacency,
):
    columns, ocean_cells = ocean_field.shape
    half_columns, atm_cells = atm_field.shape
    tiles = tile_source.shape[0]
    ocean_tiles = ocean_cells // LANES
    atm_tiles = atm_cells // LANES
    half_tiles = atm_tiles // 2
    vmem = pl.BlockSpec(memory_space=pltpu.VMEM)
    atm_out, ocean_out = pl.pallas_call(
        functools.partial(kernel, n_sfc),
        out_shape=(
            pltpu.VMEM((atm_tiles, ROWS, LANES), F32),
            pltpu.VMEM((2, ocean_tiles, ROWS, LANES), F32),
        ),
        in_specs=[pl.BlockSpec(memory_space=pltpu.HBM)] * 8,
        out_specs=(vmem, vmem),
        scratch_shapes=[
            pltpu.VMEM((ocean_tiles, ROWS, LANES), F32),
            pltpu.VMEM((ocean_tiles, ROWS, LANES), F32),
            pltpu.VMEM((2, atm_tiles, ROWS, LANES), F32),
            pltpu.VMEM((2, atm_tiles, ROWS, LANES), F32),
            pltpu.VMEM((ocean_tiles, 2, LANES), jnp.int32),
            pltpu.VMEM((2, half_tiles, 2, LANES), jnp.int32),
            pltpu.VMEM(tile_weights.shape, F32),
            pltpu.SMEM((tiles,), jnp.int32),
            pltpu.SMEM((tiles,), jnp.int32),
            pltpu.SMEM((1,), jnp.int32),
            pltpu.VMEM((2 * ocean_tiles, ROWS, LANES), jnp.int32),
            pltpu.VMEM((2 * atm_tiles, ROWS, LANES), jnp.int32),
            pltpu.VMEM((tiles, 2 * TB, LANES), BF16),
            pltpu.VMEM((tiles, ROWS, LANES), F32),
            pltpu.VMEM((tiles, 4 * ROWS, LANES), BF16),
            pltpu.VMEM((tiles, ROWS, LANES), F32),
            pltpu.VMEM((tiles, ROWS, LANES), jnp.int32),
            pltpu.VMEM((2, atm_tiles, ROWS, LANES), F32),
            pltpu.VMEM((atm_tiles, ROWS, LANES), F32),
            pltpu.VMEM((half_tiles, ROWS, LANES), F32),
            pltpu.SemaphoreType.DMA((10,)),
            pltpu.SemaphoreType.DMA((8,)),
            pltpu.SemaphoreType.DMA((8,)),
        ],
        compiler_params=pltpu.CompilerParams(
            collective_id=0, has_side_effects=True, vmem_limit_bytes=VLIM
        ),
    )(
        ocean_field.reshape(2, ROWS, ocean_tiles, LANES).transpose(0, 2, 1, 3),
        as_tiles(atm_field),
        tile_weights,
        tile_source,
        tile_target,
        tile_count,
        as_tiles(ocean_adjacency),
        as_tiles(atm_adjacency),
    )
    atm_out, ocean_out = write_out(atm_out, ocean_out)
    return (
        atm_out.transpose(1, 0, 2).reshape(half_columns, atm_cells),
        ocean_out.transpose(0, 2, 1, 3).reshape(columns, ocean_cells),
    )


def solution(mesh):
    return jax.shard_map(
        functools.partial(per_device, mesh.shape["sfc"]),
        mesh=mesh,
        in_specs=(
            P(None, ("sfc", "grp")),
            P("grp", "sfc"),
            P(("sfc", "grp"), None, None),
            P(("sfc", "grp")),
            P(("sfc", "grp")),
            P(("sfc", "grp")),
            P(None, ("sfc", "grp")),
            P(None, "sfc"),
        ),
        out_specs=(P("grp", "sfc"), P(None, ("sfc", "grp"))),
        check_vma=False,
    )
```

```python
import functools

import jax
import jax.numpy as jnp
from jax import lax
from jax.experimental import pallas as pl
from jax.experimental.pallas import tpu as pltpu
from jax.sharding import PartitionSpec as P

TB = 64
LANES = 128
ROWS = 8
GATHER = 24
JOIN = 24
VLIM = 63 * 1024 * 1024
MESH = pl.DeviceIdType.MESH
F32 = jnp.float32
BF16 = jnp.bfloat16


def roll_half(x):
    return pltpu.roll(x, TB, x.ndim - 1)


def lower_lanes(rows):
    return lax.broadcasted_iota(jnp.int32, (rows, LANES), 1) < TB


def pick_lanes(load, count, index):
    low = index & (LANES - 1)
    high = index >> 7
    bits = [(high >> b) & 1 == 1 for b in range((count - 1).bit_length())]

    def tree(first, level):
        if level < 0:
            return jnp.take_along_axis(load(first), low, axis=1, mode="promise_in_bounds")
        left = tree(first, level - 1)
        right = tree(first + (1 << level), level - 1)
        return jnp.where(bits[level], right, left)

    return tree(0, len(bits) - 1)


def stacked(x):
    high = x.astype(BF16).astype(F32)
    return jnp.concatenate([high, x - high], axis=0).astype(BF16)


def block_links(links):
    ahead = jnp.broadcast_to(links[1:2], (ROWS, LANES))
    behind = jnp.broadcast_to(links[0:1], (ROWS, LANES))
    lower = lower_lanes(ROWS)
    return (
        jnp.where(lower, ahead, roll_half(behind)),
        jnp.where(lower, roll_half(ahead), behind),
    )


def each(count, group, body):
    def step(i, carry):
        for j in range(group):
            body(i * group + j)
        return carry

    if group == count:
        step(0, 0)
    else:
        lax.fori_loop(0, count // group, step, 0)


def kernel(
    n_sfc,
    ocean_hbm,
    atm_hbm,
    weights_hbm,
    source_hbm,
    target_hbm,
    count_hbm,
    ocean_adj_hbm,
    atm_adj_hbm,
    atm_out,
    ocean_out,
    partner_ocean,
    own_ocean,
    own_fields,
    partner_fields,
    ocean_adj,
    atm_adj,
    weights,
    source,
    target,
    count,
    ocean_links,
    atm_links,
    split_weights,
    got,
    picked,
    terms,
    places,
    partial,
    from_partner,
    from_behind,
    local_sem,
    send_sem,
    recv_sem,
):
    s = lax.axis_index("sfc")
    g = lax.axis_index("grp")
    ocean_tiles = own_ocean.shape[0]
    atm_tiles = atm_hbm.shape[0]
    half_tiles = atm_tiles // 2
    tiles = weights.shape[0]
    has_following = s < n_sfc - 1
    has_before = s > 0
    following = jnp.minimum(s + 1, n_sfc - 1)
    before = jnp.maximum(s - 1, 0)
    sends_on = jnp.logical_and(g == 1, has_following)

    def local(src, dst, number):
        return pltpu.make_async_copy(src, dst, local_sem.at[number])

    def remote(src, dst, number, sfc, grp):
        return pltpu.make_async_remote_copy(
            src_ref=src,
            dst_ref=dst,
            send_sem=send_sem.at[number],
            recv_sem=recv_sem.at[number],
            device_id={"sfc": sfc, "grp": grp},
            device_id_type=MESH,
        )

    barrier = pltpu.get_barrier_semaphore()

    def greet(sfc, grp):
        pl.semaphore_signal(
            barrier, inc=1, device_id={"sfc": sfc, "grp": grp}, device_id_type=MESH
        )

    first = s == 0
    unmet = jnp.logical_and(first, g == 1)

    @pl.when(jnp.logical_not(jnp.logical_and(first, g == 0)))
    def _():
        greet(s, 1 - g)

    @pl.when(has_before)
    def _():
        greet(before, 1)

    @pl.when(sends_on)
    def _():
        greet(following, 0)
        greet(following, 1)

    small_copies = [
        local(source_hbm, source, 0),
        local(target_hbm, target, 1),
        local(count_hbm, count, 2),
        local(ocean_adj_hbm, ocean_adj, 3),
        local(ocean_hbm.at[1 - g], partner_ocean, 4),
    ]
    ocean_copy = local(ocean_hbm.at[g], own_ocean, 9)
    weights_copy = local(weights_hbm, weights, 5)
    field_copy = local(atm_hbm, own_fields.at[0], 6)
    low_adj_copy = local(atm_adj_hbm.at[pl.ds(g * half_tiles, half_tiles)], atm_adj.at[0], 7)
    high_adj_copy = local(atm_adj_hbm.at[pl.ds(half_tiles, half_tiles)], atm_adj.at[1], 8)
    for copy in small_copies + [weights_copy]:
        copy.start()

    peers = 1 - unmet.astype(jnp.int32) + has_before.astype(jnp.int32)
    pl.semaphore_wait(barrier, peers + 2 * sends_on.astype(jnp.int32))

    def partner_field(part):
        return remote(atm_hbm, partner_fields.at[0], 0, s, 1 - part)

    def before_field(part):
        landing = own_fields if part == 1 else partner_fields
        return remote(atm_hbm, landing.at[1], 1 + part, before, 1)

    def before_adjacency():
        return remote(atm_adj_hbm.at[pl.ds(0, half_tiles)], atm_adj.at[1], 3, before, 1)

    @pl.when(g == 0)
    def _():
        partner_field(0).start()

        @pl.when(has_before)
        def _():
            before_adjacency().start()

    @pl.when(g == 1)
    def _():
        @pl.when(has_before)
        def _():
            before_field(1).start()
            partner_field(1).start()

    for copy in [ocean_copy, field_copy, low_adj_copy]:
        copy.start()

    @pl.when(g == 0)
    def _():
        high_adj_copy.start()

    for copy in small_copies:
        copy.wait()

    live = count[0]
    upper = 1 - lower_lanes(ROWS).astype(jnp.int32)

    def store_links(links, first, adjacency, number):
        for k in range(number):
            even, odd = block_links(adjacency[k])
            links[first + 2 * k] = even
            links[first + 2 * k + 1] = odd

    def store_places(block_of):
        for t in range(tiles):
            places[t] = jnp.where(t < live, block_of(t), -2) - upper

    def scatter(out, part, first_tile, number):
        group = number

        def step(i, carry):
            sums = [jnp.zeros((ROWS, LANES), F32) for _ in range(group)]
            for t in range(tiles):
                place, term = places[t], terms[t]
                for j in range(group):
                    first = 2 * (first_tile + i * group + j)
                    sums[j] = sums[j] + jnp.where(place == first, term, 0.0)
            for j in range(group):
                out[part, first_tile + i * group + j] = sums[j]
            return carry

        lax.fori_loop(0, number // group, step, 0)

    def pick_ocean(ocean, group):
        for t in group:
            got[t] = pick_lanes(lambda k: ocean[k], ocean_tiles, ocean_links[source[t]])

        for t in group:
            block = source[t]
            tile = ocean[block >> 1]
            field = jnp.where(upper * 0 + (block & 1) == 0, tile, roll_half(tile))
            slope = roll_half(got[t]) - got[t]
            picked[t, : 2 * ROWS] = stacked(jnp.where(lower_lanes(ROWS), field, slope))

    def forward(group):
        for t in group[::2]:
            product = lax.dot_general(
                jnp.concatenate([picked[t, : 2 * ROWS], picked[t + 1, : 2 * ROWS]], axis=0),
                jnp.concatenate([split_weights[t], split_weights[t + 1]], axis=0),
                (((1,), (1,)), ((), ())),
                preferred_element_type=F32,
            )
            for j in range(2):
                mine = product[2 * ROWS * j : 2 * ROWS * (j + 1), LANES * j : LANES * (j + 1)]
                added = mine[:ROWS] + mine[ROWS:]
                terms[t + j] = added + roll_half(added)

    run_start = g * half_tiles * 2
    store_links(ocean_links, 0, ocean_adj, ocean_tiles)
    group_size = 24
    groups = [range(i, i + group_size) for i in range(0, tiles, group_size)]
    for group in groups:
        pick_ocean(partner_ocean, group)
        weights_copy.wait()
        for t in group:
            split_weights[t] = stacked(weights[t])
        forward(group)
    store_places(lambda t: target[t] - run_start)
    scatter(partial, 0, 0, half_tiles)

    low_half, high_half = pl.ds(0, half_tiles), pl.ds(half_tiles, half_tiles)

    def following_sum(part):
        return remote(partial.at[part, high_half], from_behind, 5 + part, following, part)

    def partner_low(part):
        return remote(partial.at[0, low_half], from_partner.at[low_half], 4, s, 1 - part)

    def partner_high():
        return remote(partial.at[0, high_half], from_partner.at[high_half], 7, s, 1)

    @pl.when(g == 0)
    def _():
        partner_low(0).start()

    @pl.when(jnp.logical_and(g == 1, has_before))
    def _():
        partner_low(1).start()

    scatter(partial, 0, half_tiles, half_tiles)

    @pl.when(g == 0)
    def _():
        partner_high().start()

        @pl.when(has_before)
        def _():
            before_field(0).start()

    @pl.when(sends_on)
    def _():
        following_sum(0).start()

    ocean_copy.wait()
    for group in groups:
        pick_ocean(own_ocean, group)
        forward(group)
    scatter(partial, 1, 0, atm_tiles)

    @pl.when(sends_on)
    def _():
        following_sum(1).start()

    is_last = jnp.logical_not(has_following).astype(jnp.int32)

    def pick_atm(fields):
        def place_of(t):
            block = jnp.clip(target[t] - run_start, 0, 2 * atm_tiles - 1)
            past = g * (block >= atm_tiles).astype(jnp.int32)
            return block, past

        def gather(t):
            block, past = place_of(t)
            got[t] = pick_lanes(
                lambda k: fields[past, k], atm_tiles, atm_links[block]
            )

        each(tiles, GATHER, gather)

        def join(t):
            block, past = place_of(t)
            tile = fields[past, (block + run_start - 2 * atm_tiles * past) >> 1]
            turned = roll_half(tile)
            lower = lower_lanes(ROWS)
            keep = upper * 0 + past * is_last == 0
            field = jnp.where(upper == (block & 1), tile, turned)
            ahead = roll_half(got[t]) - got[t]
            slope = jnp.where(lower, -ahead, ahead)
            picked[t, : 2 * ROWS] = stacked(jnp.where(keep, field, 0.0))
            picked[t, 2 * ROWS :] = stacked(jnp.where(keep, slope, 0.0))

        each(tiles, JOIN, join)

    def backward():
        lower = lower_lanes(ROWS)
        for t in range(0, tiles, 2):
            product = jnp.dot(
                jnp.concatenate([picked[t], picked[t + 1]], axis=0),
                jnp.concatenate([split_weights[t], split_weights[t + 1]], axis=1),
                preferred_element_type=F32,
            )
            for j in range(2):
                mine = product[4 * ROWS * j : 4 * ROWS * (j + 1), LANES * j : LANES * (j + 1)]
                field = mine[:ROWS] + mine[ROWS : 2 * ROWS]
                slope = mine[2 * ROWS : 3 * ROWS] + mine[3 * ROWS :]
                both = jnp.where(lower, field, slope)
                terms[t + j] = both + roll_half(both)

    low_adj_copy.wait()
    field_copy.wait()

    @pl.when(g == 0)
    def _():
        high_adj_copy.wait()

    @pl.when(sends_on)
    def _():
        before_adjacency().wait_recv()
        before_field(1).wait_recv()

    store_links(atm_links, 0, atm_adj.at[0], half_tiles)
    store_links(atm_links, 2 * half_tiles, atm_adj.at[1], half_tiles)
    store_places(lambda t: source[t])
    pick_atm(own_fields)
    backward()
    scatter(ocean_out, g, 0, ocean_tiles)

    @pl.when(g == 0)
    def _():
        partner_field(1).wait_recv()

    @pl.when(g == 1)
    def _():
        partner_field(0).wait_recv()

        @pl.when(first)
        def _():
            partner_field(1).start()
            partner_low(1).start()

    @pl.when(sends_on)
    def _():
        before_field(0).wait_recv()

    pick_atm(partner_fields)
    backward()
    scatter(ocean_out, 1 - g, 0, ocean_tiles)

    def behind_sum():
        return jnp.where(has_before, from_behind[...], 0.0)

    @pl.when(g == 0)
    def _():
        partner_low(1).wait_recv()

        @pl.when(has_before)
        def _():
            following_sum(0).wait_recv()

        atm_out[low_half] = partial[1, low_half] + behind_sum()
        atm_out[high_half] = partial[1, high_half] + from_partner[low_half]

    @pl.when(g == 1)
    def _():
        partner_low(0).wait_recv()

        @pl.when(has_before)
        def _():
            following_sum(1).wait_recv()

        atm_out[low_half] = from_partner[low_half] + behind_sum()
        partner_high().wait_recv()
        atm_out[high_half] = from_partner[high_half] + partial[1, low_half]

    @pl.when(g == 0)
    def _():
        partner_field(0).wait_send()
        partner_low(0).wait_send()
        partner_high().wait_send()

        @pl.when(has_before)
        def _():
            before_adjacency().wait_send()
            before_field(0).wait_send()

    @pl.when(g == 1)
    def _():
        partner_field(1).wait_send()
        partner_low(1).wait_send()

        @pl.when(has_before)
        def _():
            before_field(1).wait_send()

    @pl.when(sends_on)
    def _():
        following_sum(0).wait_send()
        following_sum(1).wait_send()


def as_tiles(x):
    rows, cells = x.shape
    return x.reshape(rows, cells // LANES, LANES).transpose(1, 0, 2)


def write_kernel(atm, ocean, atm_out, ocean_out, sem):
    copies = [
        pltpu.make_async_copy(atm, atm_out, sem.at[0]),
        pltpu.make_async_copy(ocean, ocean_out, sem.at[1]),
    ]
    for copy in copies:
        copy.start()
    for copy in copies:
        copy.wait()


def write_out(atm, ocean):
    return pl.pallas_call(
        write_kernel,
        out_shape=(
            jax.ShapeDtypeStruct(atm.shape, F32),
            jax.ShapeDtypeStruct(ocean.shape, F32),
        ),
        in_specs=[pl.BlockSpec(memory_space=pltpu.VMEM)] * 2,
        out_specs=[pl.BlockSpec(memory_space=pltpu.HBM)] * 2,
        scratch_shapes=[pltpu.SemaphoreType.DMA((2,))],
    )(
        pltpu.with_memory_space_constraint(atm, pltpu.VMEM),
        pltpu.with_memory_space_constraint(ocean, pltpu.VMEM),
    )


def per_device(
    n_sfc,
    ocean_field,
    atm_field,
    tile_weights,
    tile_source,
    tile_target,
    tile_count,
    ocean_adjacency,
    atm_adjacency,
):
    columns, ocean_cells = ocean_field.shape
    half_columns, atm_cells = atm_field.shape
    tiles = tile_source.shape[0]
    ocean_tiles = ocean_cells // LANES
    atm_tiles = atm_cells // LANES
    half_tiles = atm_tiles // 2
    vmem = pl.BlockSpec(memory_space=pltpu.VMEM)
    atm_out, ocean_out = pl.pallas_call(
        functools.partial(kernel, n_sfc),
        out_shape=(
            pltpu.VMEM((atm_tiles, ROWS, LANES), F32),
            pltpu.VMEM((2, ocean_tiles, ROWS, LANES), F32),
        ),
        in_specs=[pl.BlockSpec(memory_space=pltpu.HBM)] * 8,
        out_specs=(vmem, vmem),
        scratch_shapes=[
            pltpu.VMEM((ocean_tiles, ROWS, LANES), F32),
            pltpu.VMEM((ocean_tiles, ROWS, LANES), F32),
            pltpu.VMEM((2, atm_tiles, ROWS, LANES), F32),
            pltpu.VMEM((2, atm_tiles, ROWS, LANES), F32),
            pltpu.VMEM((ocean_tiles, 2, LANES), jnp.int32),
            pltpu.VMEM((2, half_tiles, 2, LANES), jnp.int32),
            pltpu.VMEM(tile_weights.shape, F32),
            pltpu.SMEM((tiles,), jnp.int32),
            pltpu.SMEM((tiles,), jnp.int32),
            pltpu.SMEM((1,), jnp.int32),
            pltpu.VMEM((2 * ocean_tiles, ROWS, LANES), jnp.int32),
            pltpu.VMEM((2 * atm_tiles, ROWS, LANES), jnp.int32),
            pltpu.VMEM((tiles, 2 * TB, LANES), BF16),
            pltpu.VMEM((tiles, ROWS, LANES), F32),
            pltpu.VMEM((tiles, 4 * ROWS, LANES), BF16),
            pltpu.VMEM((tiles, ROWS, LANES), F32),
            pltpu.VMEM((tiles, ROWS, LANES), jnp.int32),
            pltpu.VMEM((2, atm_tiles, ROWS, LANES), F32),
            pltpu.VMEM((atm_tiles, ROWS, LANES), F32),
            pltpu.VMEM((half_tiles, ROWS, LANES), F32),
            pltpu.SemaphoreType.DMA((10,)),
            pltpu.SemaphoreType.DMA((8,)),
            pltpu.SemaphoreType.DMA((8,)),
        ],
        compiler_params=pltpu.CompilerParams(
            collective_id=0, has_side_effects=True, vmem_limit_bytes=VLIM
        ),
    )(
        ocean_field.reshape(2, ROWS, ocean_tiles, LANES).transpose(0, 2, 1, 3),
        as_tiles(atm_field),
        tile_weights,
        tile_source,
        tile_target,
        tile_count,
        as_tiles(ocean_adjacency),
        as_tiles(atm_adjacency),
    )
    atm_out, ocean_out = write_out(atm_out, ocean_out)
    return (
        atm_out.transpose(1, 0, 2).reshape(half_columns, atm_cells),
        ocean_out.transpose(0, 2, 1, 3).reshape(columns, ocean_cells),
    )


def solution(mesh):
    return jax.shard_map(
        functools.partial(per_device, mesh.shape["sfc"]),
        mesh=mesh,
        in_specs=(
            P(None, ("sfc", "grp")),
            P("grp", "sfc"),
            P(("sfc", "grp"), None, None),
            P(("sfc", "grp")),
            P(("sfc", "grp")),
            P(("sfc", "grp")),
            P(None, ("sfc", "grp")),
            P(None, "sfc"),
        ),
        out_specs=(P("grp", "sfc"), P(None, ("sfc", "grp"))),
        check_vma=False,
    )
```
